256 devices in a mesh: samp: 8 (over y, core), ty: 8 (over z), tx: 4 (over x).
Axes of the slice: x: 4, y: 4, z: 8, core: 2. Of those that a mesh axis runs over, the one named last changes fastest.
Arguments:
- radiance: float32 [8, 3, 1024, 512], P('samp', None, 'ty', 'tx'), may hold values from 0 to 64
- moment: float32 [8, 1024, 512], P('samp', 'ty', 'tx'), may hold values from 0 to 128
- normal: float32 [8, 3, 1024, 512], P('samp', None, 'ty', 'tx'), may hold values from -192 to 192
- depth_sum: float32 [8, 1024, 512], P('samp', 'ty', 'tx'), may hold values from 0 to 64
- counts: int32 [8, 64, 32], P('samp', 'ty', 'tx'), may hold values from 1 to 64
Outputs:
- denoised: float32 [3, 1024, 512], P(None, 'ty', 'tx')
- variance: float32 [1024, 512], P('ty', 'tx')
The draws below stay inside these ranges and needn't reach their ends.
All inputs are finite; a program needn't handle non-finite values.
Results may differ from the reference program's by a relative error of at most 0.0001.
Values sent between devices are 32-bit elements; how exact they have to be, the bound alone decides.
No kernel may reach another device: no remote copies, remote signals or barrier semaphores. Data moves between devices by JAX's collectives and lax.ppermute only.
A program may use at most 64 MiB of HBM per device.

```python
import jax
import jax.numpy as jnp
from jax import lax

LEVELS = 4
BLK = 16
GROUPS = 8
H = 1024
W = 512


def plant(array, own_key, least, top_value):
    shape = array.shape
    index_at = [jax.random.randint(jax.random.fold_in(own_key, axis), (), 0, shape[axis]) for axis in range(len(shape))]
    array = array.at[tuple(index_at)].set(least)
    longest = shape.index(max(shape))
    index_at[longest] = (index_at[longest] + 1) % shape[longest]
    return array.at[tuple(index_at)].set(top_value)


def shard_levels(own_key, extent, pieces, smallest, top_value):
    level, own = 1.0, jax.random.fold_in(own_key, 6)
    for dim, blocks in pieces:
        steps = jnp.exp(jax.random.uniform(jax.random.fold_in(own, dim), (blocks,), jnp.float32, smallest / len(pieces), top_value / len(pieces)))
        level = level * jnp.repeat(steps, extent[dim] // blocks).reshape([-1 if axis == dim else 1 for axis in range(len(extent))])
    return level


def centred(key, shape, deviation, most, cuts=(), dtype=jnp.bfloat16):
    array = deviation * jax.random.normal(key, shape, jnp.float32)
    if cuts:
        array = array * shard_levels(key, shape, cuts, -0.22, 0.18)
    return jnp.clip(array, -most, most).astype(dtype)


def setup_inputs(seed: int = 0) -> dict:
    key_list = jax.random.split(jax.random.key(seed), 6)
    radiance = jnp.clip(64.0 * jax.random.uniform(key_list[0], (GROUPS, 3, H, W), jnp.float32) ** shard_levels(key_list[0], (GROUPS, 3, H, W), ((0, 8), (2, 8), (3, 4)), -0.2, 0.2), 0.0, 64.0)
    moment = jnp.clip(128.0 * jax.random.uniform(key_list[1], (GROUPS, H, W), jnp.float32) ** shard_levels(key_list[1], (GROUPS, H, W), ((0, 8), (1, 8), (2, 4)), -0.2, 0.2), 0.0, 128.0)
    normal = centred(key_list[2], (GROUPS, 3, H, W), 32.0, 192.0, ((0, 8), (2, 8), (3, 4)), jnp.float32)
    depth_sum = jnp.clip(64.0 * jax.random.uniform(key_list[3], (GROUPS, H, W), jnp.float32) ** shard_levels(key_list[3], (GROUPS, H, W), ((0, 8), (1, 8), (2, 4)), -0.2, 0.2), 0.0, 64.0)
    counts = plant(jax.random.randint(key_list[4], (GROUPS, H // BLK, W // BLK), 1, 65), jax.random.fold_in(key_list[4], 1), 1, 64).astype(jnp.int32)
    return {"radiance": radiance, "moment": moment, "normal": normal, "depth_sum": depth_sum, "counts": counts}


TAPS = (0.0625, 0.25, 0.375, 0.25, 0.0625)
SIGMA_DEPTH = 0.5
SIGMA_NORMAL = 1.0
SIGMA_LUMA = 4.0
LUMA_FLOOR = 0.5

def luminance(colour):
    return 0.2126 * colour[0] + 0.7152 * colour[1] + 0.0722 * colour[2]

def atrous_level(colour_pad, var_pad, normal_pad, depth_pad, inside_pad, dilation, height, breadth):
    rim_rows = 2 * dilation

    def centre(source):
        return source[..., rim_rows:rim_rows + height, rim_rows:rim_rows + breadth]
    colour_mid = centre(colour_pad)
    normal_mid = centre(normal_pad)
    depth_mid = centre(depth_pad)
    luma_mid = luminance(colour_mid)
    spread = SIGMA_LUMA * jnp.sqrt(centre(var_pad)) + LUMA_FLOOR
    weight_sum = jnp.zeros((height, breadth), jnp.float32)
    colour_acc = jnp.zeros((3, height, breadth), jnp.float32)
    var_acc = jnp.zeros((height, breadth), jnp.float32)
    for tap_row in range(5):
        for tap_col in range(5):
            top_row = tap_row * dilation
            left_col = tap_col * dilation

            def window(source):
                return source[..., top_row:top_row + height, left_col:left_col + breadth]
            colour_tap = window(colour_pad)
            exponent = jnp.abs(window(depth_pad) - depth_mid) / SIGMA_DEPTH
            exponent = exponent + lax.optimization_barrier(jnp.sum(jnp.square(window(normal_pad) - normal_mid), axis=0)) / SIGMA_NORMAL
            exponent = exponent + jnp.abs(luminance(colour_tap) - luma_mid) / spread
            weight = TAPS[tap_row] * TAPS[tap_col] * window(inside_pad) * jnp.exp(-exponent)
            weight_sum = weight_sum + weight
            colour_acc = colour_acc + weight[None] * colour_tap
            var_acc = var_acc + weight * weight * window(var_pad)
    return (colour_acc / weight_sum[None], var_acc / (weight_sum * weight_sum))

def reference(radiance, moment, normal, depth_sum, counts):
    totals = jnp.concatenate([lax.optimization_barrier(jnp.sum(radiance, axis=0)), lax.optimization_barrier(jnp.sum(moment, axis=0))[None], lax.optimization_barrier(jnp.sum(normal, axis=0)), lax.optimization_barrier(jnp.sum(depth_sum, axis=0))[None]], axis=0)
    samples = lax.optimization_barrier(jnp.sum(counts.astype(jnp.float32), axis=0))
    samples = jnp.repeat(jnp.repeat(samples, BLK, axis=0), BLK, axis=1)
    mean_values = totals / samples[None]
    colour = mean_values[0:3]
    second = mean_values[3]
    normals = mean_values[4:7]
    depth_map = mean_values[7]
    variance = jnp.maximum(second - jnp.square(luminance(colour)), 0.0)
    inside = jnp.ones((H, W), jnp.float32)
    for level_idx in range(LEVELS):
        dilation = 2 ** level_idx
        rim_rows = 2 * dilation
        pad_three = ((0, 0), (rim_rows, rim_rows), (rim_rows, rim_rows))
        colour, variance = atrous_level(jnp.pad(colour, pad_three), jnp.pad(variance, rim_rows), jnp.pad(normals, pad_three), jnp.pad(depth_map, rim_rows), jnp.pad(inside, rim_rows), dilation, H, W)
    return (colour, variance)
```

```python
import functools

import jax
import jax.numpy as jnp
from jax import lax
from jax.experimental import pallas as pl
from jax.experimental.pallas import tpu as pltpu
from jax.sharding import PartitionSpec as P

TAPS = (0.0625, 0.25, 0.375, 0.25, 0.0625)
LUMA = (0.2126, 0.7152, 0.0722)
SIGMA_DEPTH = 0.5
SIGMA_NORMAL = 1.0
SIGMA_LUMA = 4.0
LUMA_FLOOR = 0.5
FAR = 1e30

TILE = 128
HALF = 64
RIM = 32
WIN = 96
BLK = 16
AXES = ("samp", "ty", "tx")


def place():
    samp = lax.axis_index("samp")
    ty = lax.axis_index("ty")
    tx = lax.axis_index("tx")
    core = lax.rem(samp, 2)
    y = samp // 2
    half_row = lax.rem(y // 2 + ty, 2)
    half_col = lax.rem(lax.rem(y, 2) + tx, 2)
    return core, half_row, half_col, ty, tx


def luminance(c0, c1, c2):
    return LUMA[0] * c0 + LUMA[1] * c1 + LUMA[2] * c2


def rows(start, count):
    return pl.ds(start, count)


def aligned(value):
    return pl.multiple_of(value, 8)


def pack_kernel(rad, mom, nor, dep, cnt, keep, send):
    core = place()[0]

    def fill(colour_ref, normal_ref):
        for ch in range(3):
            colour_ref[ch * TILE : (ch + 1) * TILE, :] = rad[0, ch]
            normal_ref[ch * TILE : (ch + 1) * TILE, :] = nor[0, ch]
        colour_ref[3 * TILE : 4 * TILE, :] = mom[0]
        normal_ref[3 * TILE : 4 * TILE, :] = dep[0]

    @pl.when(core == 0)
    def _():
        fill(keep, send)

    @pl.when(core == 1)
    def _():
        fill(send, keep)

    blocks = cnt[0].astype(jnp.float32)
    for ref in (keep, send):
        ref[4 * TILE :, :] = jnp.zeros((8, TILE), jnp.float32)
        ref[4 * TILE :, 0:8] = blocks


def pair_kernel(keep, recv, near, far):
    half_row = place()[1]
    for ref, part in ((near, half_row), (far, 1 - half_row)):
        for ch in range(4):
            at = rows(aligned(ch * TILE + 32 * part), WIN)
            ref[ch * WIN : (ch + 1) * WIN, :] = keep[at, :] + recv[at, :]
        ref[4 * WIN :, :] = keep[4 * TILE :, :] + recv[4 * TILE :, :]


def mean_kernel(own, r1, r2, r3, field, rim_x, rim_z, rim_d, samples):
    core, half_row, half_col, _, _ = place()
    lane = lax.broadcasted_iota(jnp.int32, (8, TILE), 1)

    def total(at):
        return (own[at, :] + r1[at, :]) + (r2[at, :] + r3[at, :])

    blocks = total(rows(4 * WIN, 8))
    spread = jnp.zeros((8, TILE), jnp.float32)
    for j in range(8):
        spread = jnp.where(lane // BLK == j, blocks[:, j : j + 1], spread)
    samples[...] = spread
    for i in range(WIN // BLK):
        count = jnp.broadcast_to(samples[rows(2 * half_row + i, 1), :], (BLK, TILE))
        mean = [total(rows(ch * WIN + i * BLK, BLK)) / count for ch in range(4)]
        variance = jnp.maximum(mean[3] - jnp.square(luminance(*mean[:3])), 0.0)
        mean[3] = jnp.where(core == 0, variance, mean[3])
        for ch in range(4):
            field[rows(ch * WIN + i * BLK, BLK), :] = mean[ch]
        lanes = lax.broadcasted_iota(jnp.int32, (BLK, TILE), 1)
        packed = jnp.zeros((BLK, TILE), jnp.float32)
        for ch in range(4):
            moved = pltpu.roll(mean[ch], lax.rem(32 * ch + TILE - 96 * half_col, TILE), 1)
            packed = jnp.where(lanes // 32 == ch, moved, packed)
        rim_x[rows(i * BLK, BLK), :] = packed
    first = aligned(64 * half_row)
    for ch in range(4):
        rim_z[ch * RIM : (ch + 1) * RIM, :] = field[rows(aligned(ch * WIN + first), RIM), :]
    rim_d[...] = rim_x[rows(first, RIM), :]


NF = 9
PAD = 32


def filter_kernel(*refs):
    (f0, x0, z0, d0, f1, x1, z1, d1, out, cur, geo, shifted) = refs
    core, half_row, half_col, ty, tx = place()
    lanes = lax.broadcasted_iota(jnp.int32, (RIM, TILE), 1)
    n_ty, n_tx = lax.axis_size("ty"), lax.axis_size("tx")
    x_out = ((half_col == 0) & (tx == 0)) | ((half_col == 1) & (tx == n_tx - 1))
    z_out = ((half_row == 0) & (ty == 0)) | ((half_row == 1) & (ty == n_ty - 1))
    rim_lane = (lanes // 32) == 3 * half_col
    into = jnp.where(half_col == 0, 32, 96)
    rim_at = 96 * half_col

    def cell(body, rim, ch):
        return jnp.where(
            rim_lane,
            pltpu.roll(rim, lax.rem(rim_at + TILE - 32 * ch, TILE), 1),
            pltpu.roll(body, into, 1),
        )

    body_row = PAD + 32 * (1 - half_row) - 32 * core
    edge_row = PAD + 96 * half_row - 32 * core

    def assemble(is_geo, f, x, z, d):
        for ch in range(4):
            for part in range(4):
                if part < 3:
                    value = cell(
                        f[ch * WIN + part * RIM : ch * WIN + (part + 1) * RIM, :],
                        x[part * RIM : (part + 1) * RIM, :],
                        ch,
                    )
                    at = rows(aligned(body_row + part * RIM), RIM)
                else:
                    value = cell(z[ch * RIM : (ch + 1) * RIM, :], d[...], ch)
                    at = rows(aligned(edge_row), RIM)
                if is_geo:
                    if ch == 3:
                        value = value * (1.0 / SIGMA_DEPTH)
                        outside = rim_lane & x_out
                        if part == 3:
                            outside = outside | z_out
                        value = jnp.where(outside, FAR, value)
                    geo[ch, at, :] = value
                else:
                    cur[0, ch, at, :] = value

    @pl.when(core == 0)
    def _():
        assemble(False, f0, x0, z0, d0)
        assemble(True, f1, x1, z1, d1)

    @pl.when(core == 1)
    def _():
        assemble(True, f0, x0, z0, d0)
        assemble(False, f1, x1, z1, d1)

    def add_luma(i, carry):
        at = rows(aligned(i * 8), 8)
        cur[0, 4, at, :] = luminance(cur[0, 0, at, :], cur[0, 1, at, :], cur[0, 2, at, :])
        return carry

    lax.fori_loop(0, (WIN + 2 * PAD) // 8, add_luma, 0)

    for level, (low, high) in enumerate(((0, 96), (8, 88), (16, 80), (32, 64))):
        dil = 2**level
        src, dst = level % 2, 1 - level % 2
        reach = -(-2 * dil // 8) * 8
        start, stop = PAD + low - reach, PAD + high + reach

        def shift(i, carry, src=src, start=start, dil=dil):
            at = rows(aligned(start + i * 8), 8)
            for f in range(NF):
                value = geo[f, at, :] if f < 4 else cur[src, f - 4, at, :]
                for b in range(5):
                    moved = value if b == 2 else pltpu.roll(value, (-(b - 2) * dil) % TILE, 1)
                    shifted[b, f, at, :] = moved
            return carry

        lax.fori_loop(0, (stop - start) // 8, shift, 0)

        def step(i, carry, src=src, dst=dst, low=low, dil=dil, level=level):
            base = PAD + low + i * 8
            here = rows(aligned(base), 8)
            n0, n1, n2, depth = (geo[f, here, :] for f in range(4))
            luma = cur[src, 4, here, :]
            slope = -1.0 / (SIGMA_LUMA * jnp.sqrt(cur[src, 3, here, :]) + LUMA_FLOOR)
            total = c0 = c1 = c2 = var = None
            for a in range(5):
                for b in range(5):
                    at = rows(base + (a - 2) * dil, 8)
                    tap = [shifted[b, f, at, :] for f in range(NF)]
                    e = jnp.abs(tap[8] - luma) * slope - jnp.abs(tap[3] - depth)
                    e = e - jnp.square(tap[0] - n0) - jnp.square(tap[1] - n1)
                    e = e - jnp.square(tap[2] - n2)
                    w = (TAPS[a] * TAPS[b]) * jnp.exp(e)
                    parts = (w, w * tap[4], w * tap[5], w * tap[6], w * w * tap[7])
                    if total is None:
                        total, c0, c1, c2, var = parts
                    else:
                        total, c0, c1, c2, var = (
                            p + q for p, q in zip((total, c0, c1, c2, var), parts)
                        )
            inv = 1.0 / total
            c0, c1, c2, var = c0 * inv, c1 * inv, c2 * inv, var * (inv * inv)
            if level < 3:
                for f, value in enumerate((c0, c1, c2, var, luminance(c0, c1, c2))):
                    cur[dst, f, here, :] = value
            else:
                lane = lax.broadcasted_iota(jnp.int32, (8, TILE), 1)
                for k, (p, q) in enumerate(((c0, c1), (c2, var))):
                    out[rows(aligned(k * 32 + i * 8), 8), :] = jnp.where(
                        lane < HALF, pltpu.roll(p, TILE - 32, 1), pltpu.roll(q, 32, 1)
                    )
            return carry

        lax.fori_loop(0, (high - low) // 8, step, 0)


def tile_kernel(*refs):
    ins, colour, variance = refs[:8], refs[8], refs[9]
    core, half_row, half_col, _, _ = place()
    lane = lax.broadcasted_iota(jnp.int32, (32, TILE), 1)
    low = lane < HALF
    for side in range(2):
        which = core if side == 0 else 1 - core
        for r in range(2):
            row = aligned(64 * (half_row if r == 0 else 1 - half_row) + 32 * which)
            near, other = ins[side * 4 + 2 * r], ins[side * 4 + 2 * r + 1]
            for k in range(2):
                p, q = near[k * 32 : (k + 1) * 32, :], other[k * 32 : (k + 1) * 32, :]
                left = jnp.where(half_col == 0, p, q)
                right = jnp.where(half_col == 0, q, p)
                first = jnp.where(low, left, pltpu.roll(right, HALF, 1))
                second = jnp.where(low, pltpu.roll(left, HALF, 1), right)
                at = rows(row, 32)
                colour[2 * k, at, :] = first
                if k == 0:
                    colour[1, at, :] = second
                else:
                    variance[at, :] = second


def call(kernel, shapes, scratch=()):
    return pl.pallas_call(
        kernel,
        out_shape=[jax.ShapeDtypeStruct(s, jnp.float32) for s in shapes],
        scratch_shapes=list(scratch),
        compiler_params=pltpu.CompilerParams(vmem_limit_bytes=24 * 2**20),
    )


def pairs(sizes, partner):
    n_samp, n_ty, n_tx = sizes
    out = []
    for samp in range(n_samp):
        for ty in range(n_ty):
            for tx in range(n_tx):
                to = partner(samp, ty, tx)
                if 0 <= to[1] < n_ty and 0 <= to[2] < n_tx:
                    out.append(
                        ((samp * n_ty + ty) * n_tx + tx, (to[0] * n_ty + to[1]) * n_tx + to[2])
                    )
    return out


def step_of(samp, ty, tx):
    y = samp // 2
    row = 1 if (y // 2 + ty) % 2 else -1
    col = 1 if (y % 2 + tx) % 2 else -1
    return row, col


def per_device(sizes, radiance, moment, normal, depth_sum, counts):
    def send(value, partner):
        return lax.ppermute(value, AXES, pairs(sizes, partner))

    def other_core(value):
        return send(value, lambda s, ty, tx: (s ^ 1, ty, tx))

    def other_y(value, k):
        return send(value, lambda s, ty, tx: (s ^ (2 * k), ty, tx))

    packed = (4 * TILE + 8, TILE)
    window = (4 * WIN + 8, TILE)
    keep, give = call(pack_kernel, [packed, packed])(radiance, moment, normal, depth_sum, counts)
    near, far = call(pair_kernel, [window, window])(keep, other_core(give))
    r1, r2, r3 = other_y(near, 1), other_y(far, 2), other_y(far, 3)
    field, rim_x, rim_z, rim_d = call(
        mean_kernel,
        [(4 * WIN, TILE), (WIN, TILE), (4 * RIM, TILE), (RIM, TILE)],
        [pltpu.VMEM((8, TILE), jnp.float32)],
    )(near, r1, r2, r3)
    field_1 = other_core(field)
    rim_x = send(rim_x, lambda s, ty, tx: (s, ty, tx + step_of(s, ty, tx)[1]))
    rim_z = send(rim_z, lambda s, ty, tx: (s, ty + step_of(s, ty, tx)[0], tx))
    rim_d = send(
        rim_d, lambda s, ty, tx: (s, ty + step_of(s, ty, tx)[0], tx + step_of(s, ty, tx)[1])
    )
    rims = (rim_x, rim_z, rim_d)
    rims_1 = [other_core(r) for r in rims]
    (mine,) = call(
        filter_kernel,
        [(HALF, TILE)],
        [
            pltpu.VMEM((2, 5, WIN + 2 * PAD, TILE), jnp.float32),
            pltpu.VMEM((4, WIN + 2 * PAD, TILE), jnp.float32),
            pltpu.VMEM((5, NF, WIN + 2 * PAD, TILE), jnp.float32),
        ],
    )(field, *rims, field_1, *rims_1)
    got = [mine] + [other_y(mine, k) for k in (1, 2, 3)]
    theirs = [other_core(g) for g in got]
    return tuple(call(tile_kernel, [(3, TILE, TILE), (TILE, TILE)])(*got, *theirs))


def solution(mesh):
    sizes = tuple(mesh.shape[axis] for axis in AXES)
    placed = (
        P("samp", None, "ty", "tx"),
        P("samp", "ty", "tx"),
        P("samp", None, "ty", "tx"),
        P("samp", "ty", "tx"),
        P("samp", "ty", "tx"),
    )
    return jax.shard_map(
        functools.partial(per_device, sizes),
        mesh=mesh,
        in_specs=placed,
        out_specs=(P(None, "ty", "tx"), P("ty", "tx")),
        check_vma=False,
    )
```

```python
import functools

import jax
import jax.numpy as jnp
from jax import lax
from jax.experimental import pallas as pl
from jax.experimental.pallas import tpu as pltpu
from jax.sharding import PartitionSpec as P

TAPS = (0.0625, 0.25, 0.375, 0.25, 0.0625)
LUMA = (0.2126, 0.7152, 0.0722)
SIGMA_DEPTH = 0.5
SIGMA_NORMAL = 1.0
SIGMA_LUMA = 4.0
LUMA_FLOOR = 0.5
FAR = 1e30

TILE = 128
HALF = 64
RIM = 32
WIN = 96
BLK = 16
AXES = ("samp", "ty", "tx")


def place():
    samp = lax.axis_index("samp")
    ty = lax.axis_index("ty")
    tx = lax.axis_index("tx")
    core = lax.rem(samp, 2)
    y = samp // 2
    half_row = lax.rem(y // 2 + ty, 2)
    half_col = lax.rem(lax.rem(y, 2) + tx, 2)
    return core, half_row, half_col, ty, tx


def luminance(c0, c1, c2):
    return LUMA[0] * c0 + LUMA[1] * c1 + LUMA[2] * c2


def rows(start, count):
    return pl.ds(start, count)


def aligned(value):
    return pl.multiple_of(value, 8)


def pack_kernel(rad, mom, nor, dep, cnt, keep, send, blocks, sems):
    core = place()[0]
    count = pltpu.make_async_copy(cnt.at[0], blocks, sems.at[8])
    count.start()

    def fill(colour_ref, normal_ref):
        copies = []
        for ch in range(4):
            at = rows(ch * TILE, TILE)
            colour, normal = (rad.at[0, ch], nor.at[0, ch]) if ch < 3 else (mom.at[0], dep.at[0])
            copies.append(pltpu.make_async_copy(colour, colour_ref.at[at, :], sems.at[ch]))
            copies.append(pltpu.make_async_copy(normal, normal_ref.at[at, :], sems.at[4 + ch]))
        for copy in copies:
            copy.start()
        for copy in copies:
            copy.wait()

    @pl.when(core == 0)
    def _():
        fill(keep, send)

    @pl.when(core == 1)
    def _():
        fill(send, keep)

    count.wait()
    number = blocks[...].astype(jnp.float32)
    for ref in (keep, send):
        ref[4 * TILE :, :] = jnp.zeros((8, TILE), jnp.float32)
        ref[4 * TILE :, 0:8] = number


def pair_kernel(keep, recv, near, far):
    half_row = place()[1]
    for ref, part in ((near, half_row), (far, 1 - half_row)):
        for ch in range(4):
            at = rows(aligned(ch * TILE + 32 * part), WIN)
            ref[ch * WIN : (ch + 1) * WIN, :] = keep[at, :] + recv[at, :]
        ref[4 * WIN :, :] = keep[4 * TILE :, :] + recv[4 * TILE :, :]


def mean_kernel(own, r1, r2, r3, field, rim_x, rim_z, rim_d, samples):
    core, half_row, half_col, _, _ = place()
    lane = lax.broadcasted_iota(jnp.int32, (8, TILE), 1)

    def total(at):
        return (own[at, :] + r1[at, :]) + (r2[at, :] + r3[at, :])

    blocks = total(rows(4 * WIN, 8))
    spread = jnp.zeros((8, TILE), jnp.float32)
    for j in range(8):
        spread = jnp.where(lane // BLK == j, blocks[:, j : j + 1], spread)
    samples[...] = spread
    for i in range(WIN // BLK):
        count = jnp.broadcast_to(samples[rows(2 * half_row + i, 1), :], (BLK, TILE))
        mean = [total(rows(ch * WIN + i * BLK, BLK)) / count for ch in range(4)]
        variance = jnp.maximum(mean[3] - jnp.square(luminance(*mean[:3])), 0.0)
        mean[3] = jnp.where(core == 0, variance, mean[3])
        for ch in range(4):
            field[rows(ch * WIN + i * BLK, BLK), :] = mean[ch]
        lanes = lax.broadcasted_iota(jnp.int32, (BLK, TILE), 1)
        packed = jnp.zeros((BLK, TILE), jnp.float32)
        for ch in range(4):
            moved = pltpu.roll(mean[ch], lax.rem(32 * ch + TILE - 96 * half_col, TILE), 1)
            packed = jnp.where(lanes // 32 == ch, moved, packed)
        rim_x[rows(i * BLK, BLK), :] = packed
    first = aligned(64 * half_row)
    for ch in range(4):
        rim_z[ch * RIM : (ch + 1) * RIM, :] = field[rows(aligned(ch * WIN + first), RIM), :]
    rim_d[...] = rim_x[rows(first, RIM), :]


SPANS = ((0, 96), (8, 88), (16, 80), (32, 64))
PAD = 32


def filter_kernel(*refs):
    (f0, x0, z0, d0, f1, x1, z1, d1, out, cur, geo, cur_moved, geo_moved) = refs
    core, half_row, half_col, ty, tx = place()
    lanes = lax.broadcasted_iota(jnp.int32, (RIM, TILE), 1)
    n_ty, n_tx = lax.axis_size("ty"), lax.axis_size("tx")
    x_out = ((half_col == 0) & (tx == 0)) | ((half_col == 1) & (tx == n_tx - 1))
    z_out = ((half_row == 0) & (ty == 0)) | ((half_row == 1) & (ty == n_ty - 1))
    rim_lane = (lanes // 32) == 3 * half_col
    into = jnp.where(half_col == 0, 32, 96)
    rim_at = 96 * half_col

    def cell(body, rim, ch):
        return jnp.where(
            rim_lane,
            pltpu.roll(rim, lax.rem(rim_at + TILE - 32 * ch, TILE), 1),
            pltpu.roll(body, into, 1),
        )

    body_row = PAD + 32 * (1 - half_row) - 32 * core
    edge_row = PAD + 96 * half_row - 32 * core

    def assemble(is_geo, f, x, z, d):
        for ch in range(4):
            for part in range(4):
                if part < 3:
                    value = cell(
                        f[ch * WIN + part * RIM : ch * WIN + (part + 1) * RIM, :],
                        x[part * RIM : (part + 1) * RIM, :],
                        ch,
                    )
                    at = rows(aligned(body_row + part * RIM), RIM)
                else:
                    value = cell(z[ch * RIM : (ch + 1) * RIM, :], d[...], ch)
                    at = rows(aligned(edge_row), RIM)
                if is_geo:
                    if ch == 3:
                        value = value * (1.0 / SIGMA_DEPTH)
                        outside = rim_lane & x_out
                        if part == 3:
                            outside = outside | z_out
                        value = jnp.where(outside, FAR, value)
                    geo[ch, at, :] = value
                else:
                    cur[0, ch, at, :] = value

    @pl.when(core == 0)
    def _():
        assemble(False, f0, x0, z0, d0)
        assemble(True, f1, x1, z1, d1)

    @pl.when(core == 1)
    def _():
        assemble(True, f0, x0, z0, d0)
        assemble(False, f1, x1, z1, d1)

    for r in range(PAD, PAD + WIN, 8):
        at = rows(r, 8)
        cur[0, 4, at, :] = luminance(cur[0, 0, at, :], cur[0, 1, at, :], cur[0, 2, at, :])

    moved_by = (-16, -8, -4, -2, -1, 1, 2, 4, 8, 16)
    made = set()

    def roll(value, by):
        return pltpu.roll(value, -by % TILE, 1)

    for level, (low, high) in enumerate(SPANS):
        dil = 2**level
        src, dst = level % 2, 1 - level % 2
        reach = -(-2 * dil // 8) * 8
        start, stop = PAD + max(low - reach, 0), PAD + min(high + reach, WIN)
        for r in range(start, stop, 8):
            at = rows(r, 8)
            for b in (-2, -1, 1, 2):
                if (b * dil, r) not in made:
                    made.add((b * dil, r))
                    for f in range(4):
                        geo_moved[moved_by.index(b * dil), f, at, :] = roll(geo[f, at, :], b * dil)
                moved = [roll(cur[src, f, at, :], b * dil) for f in range(4)]
                moved.append(luminance(*moved[:3]))
                for f in range(5):
                    cur_moved[b + 2, f, at, :] = moved[f]

        for r in range(PAD + low, PAD + high, 8):
            here = rows(r, 8)
            n0, n1, n2, depth = (geo[f, here, :] for f in range(4))
            luma = cur[src, 4, here, :]
            slope = -1.0 / (SIGMA_LUMA * jnp.sqrt(cur[src, 3, here, :]) + LUMA_FLOOR)
            sums = None
            for a in range(-2, 3):
                at = rows(r + a * dil, 8)
                for b in range(-2, 3):
                    if b == 0:
                        g = [geo[f, at, :] for f in range(4)]
                        t = [cur[src, f, at, :] for f in range(5)]
                    else:
                        g = [geo_moved[moved_by.index(b * dil), f, at, :] for f in range(4)]
                        t = [cur_moved[b + 2, f, at, :] for f in range(5)]
                    e = jnp.abs(t[4] - luma) * slope - jnp.abs(g[3] - depth)
                    e = e - jnp.square(g[0] - n0) - jnp.square(g[1] - n1)
                    e = e - jnp.square(g[2] - n2)
                    w = (TAPS[a + 2] * TAPS[b + 2]) * jnp.exp(e)
                    parts = (w, w * t[0], w * t[1], w * t[2], w * w * t[3])
                    sums = parts if sums is None else [p + q for p, q in zip(sums, parts)]
            inv = 1.0 / sums[0]
            c0, c1, c2, var = sums[1] * inv, sums[2] * inv, sums[3] * inv, sums[4] * (inv * inv)
            if level < len(SPANS) - 1:
                for f, value in enumerate((c0, c1, c2, var, luminance(c0, c1, c2))):
                    cur[dst, f, here, :] = value
            else:
                lane = lax.broadcasted_iota(jnp.int32, (8, TILE), 1)
                for k, (p, q) in enumerate(((c0, c1), (c2, var))):
                    out[rows(k * 32 + r - PAD - low, 8), :] = jnp.where(
                        lane < HALF, roll(p, 32), roll(q, -32)
                    )


def tile_kernel(*refs):
    ins, colour, variance = refs[:8], refs[8], refs[9]
    core, half_row, half_col, _, _ = place()
    lane = lax.broadcasted_iota(jnp.int32, (32, TILE), 1)
    low = lane < HALF
    for side in range(2):
        which = core if side == 0 else 1 - core
        for r in range(2):
            row = aligned(64 * (half_row if r == 0 else 1 - half_row) + 32 * which)
            near, other = ins[side * 4 + 2 * r], ins[side * 4 + 2 * r + 1]
            for k in range(2):
                p, q = near[k * 32 : (k + 1) * 32, :], other[k * 32 : (k + 1) * 32, :]
                left = jnp.where(half_col == 0, p, q)
                right = jnp.where(half_col == 0, q, p)
                first = jnp.where(low, left, pltpu.roll(right, HALF, 1))
                second = jnp.where(low, pltpu.roll(left, HALF, 1), right)
                at = rows(row, 32)
                colour[2 * k, at, :] = first
                if k == 0:
                    colour[1, at, :] = second
                else:
                    variance[at, :] = second


def call(kernel, shapes, scratch=(), space=None):
    return pl.pallas_call(
        kernel,
        **({"in_specs": [pl.BlockSpec(memory_space=pltpu.HBM)] * space} if space else {}),
        out_shape=[jax.ShapeDtypeStruct(s, jnp.float32) for s in shapes],
        scratch_shapes=list(scratch),
        compiler_params=pltpu.CompilerParams(vmem_limit_bytes=24 * 2**20),
    )


def pairs(sizes, partner):
    n_samp, n_ty, n_tx = sizes
    out = []
    for samp in range(n_samp):
        for ty in range(n_ty):
            for tx in range(n_tx):
                to = partner(samp, ty, tx)
                if 0 <= to[1] < n_ty and 0 <= to[2] < n_tx:
                    out.append(
                        ((samp * n_ty + ty) * n_tx + tx, (to[0] * n_ty + to[1]) * n_tx + to[2])
                    )
    return out


def step_of(samp, ty, tx):
    y = samp // 2
    row = 1 if (y // 2 + ty) % 2 else -1
    col = 1 if (y % 2 + tx) % 2 else -1
    return row, col


def per_device(sizes, radiance, moment, normal, depth_sum, counts):
    def send(value, partner):
        return lax.ppermute(value, AXES, pairs(sizes, partner))

    def other_core(value):
        return send(value, lambda s, ty, tx: (s ^ 1, ty, tx))

    def other_y(value, k):
        return send(value, lambda s, ty, tx: (s ^ (2 * k), ty, tx))

    packed = (4 * TILE + 8, TILE)
    window = (4 * WIN + 8, TILE)
    keep, give = call(
        pack_kernel,
        [packed, packed],
        [pltpu.VMEM((8, 8), jnp.int32), pltpu.SemaphoreType.DMA((9,))],
        5,
    )(
        *(
            pltpu.with_memory_space_constraint(value, pltpu.HBM)
            for value in (radiance, moment, normal, depth_sum, counts)
        )
    )
    near, far = call(pair_kernel, [window, window])(keep, other_core(give))
    r1, r2, r3 = other_y(near, 1), other_y(far, 2), other_y(far, 3)
    field, rim_x, rim_z, rim_d = call(
        mean_kernel,
        [(4 * WIN, TILE), (WIN, TILE), (4 * RIM, TILE), (RIM, TILE)],
        [pltpu.VMEM((8, TILE), jnp.float32)],
    )(near, r1, r2, r3)
    field_1 = other_core(field)
    rim_x = send(rim_x, lambda s, ty, tx: (s, ty, tx + step_of(s, ty, tx)[1]))
    rim_z = send(rim_z, lambda s, ty, tx: (s, ty + step_of(s, ty, tx)[0], tx))
    rim_d = send(
        rim_d, lambda s, ty, tx: (s, ty + step_of(s, ty, tx)[0], tx + step_of(s, ty, tx)[1])
    )
    rims = lax.optimization_barrier((rim_x, rim_z, rim_d))
    rims_1 = [other_core(r) for r in rims]
    (mine,) = call(
        filter_kernel,
        [(HALF, TILE)],
        [
            pltpu.VMEM((2, 5, WIN + 2 * PAD, TILE), jnp.float32),
            pltpu.VMEM((4, WIN + 2 * PAD, TILE), jnp.float32),
            pltpu.VMEM((5, 5, WIN + 2 * PAD, TILE), jnp.float32),
            pltpu.VMEM((10, 4, WIN + 2 * PAD, TILE), jnp.float32),
        ],
    )(field, *rims, field_1, *rims_1)
    got = [mine] + [other_y(mine, k) for k in (1, 2, 3)]
    theirs = [other_core(g) for g in got]
    return tuple(call(tile_kernel, [(3, TILE, TILE), (TILE, TILE)])(*got, *theirs))


def solution(mesh):
    sizes = tuple(mesh.shape[axis] for axis in AXES)
    placed = (
        P("samp", None, "ty", "tx"),
        P("samp", "ty", "tx"),
        P("samp", None, "ty", "tx"),
        P("samp", "ty", "tx"),
        P("samp", "ty", "tx"),
    )
    return jax.shard_map(
        functools.partial(per_device, sizes),
        mesh=mesh,
        in_specs=placed,
        out_specs=(P(None, "ty", "tx"), P("ty", "tx")),
        check_vma=False,
    )
```

```python
import functools

import jax
import jax.numpy as jnp
from jax import lax
from jax.experimental import pallas as pl
from jax.experimental.pallas import tpu as pltpu
from jax.sharding import PartitionSpec as P

TAPS = (0.0625, 0.25, 0.375, 0.25, 0.0625)
LUMA = (0.2126, 0.7152, 0.0722)
SIGMA_DEPTH = 0.5
SIGMA_NORMAL = 1.0
SIGMA_LUMA = 4.0
LUMA_FLOOR = 0.5
FAR = 1e30

TILE = 128
HALF = 64
RIM = 32
WIN = 96
BLK = 16
AXES = ("samp", "ty", "tx")


def place():
    samp = lax.axis_index("samp")
    ty = lax.axis_index("ty")
    tx = lax.axis_index("tx")
    core = lax.rem(samp, 2)
    y = samp // 2
    half_row = lax.rem(y // 2 + ty, 2)
    half_col = lax.rem(lax.rem(y + 1, 4) // 2 + tx, 2)
    return core, half_row, half_col, ty, tx


def luminance(c0, c1, c2):
    return LUMA[0] * c0 + LUMA[1] * c1 + LUMA[2] * c2


def rows(start, count):
    return pl.ds(start, count)


def aligned(value):
    return pl.multiple_of(value, 8)


def pack_kernel(rad, mom, nor, dep, cnt, keep, send, blocks, sems):
    core = place()[0]
    count = pltpu.make_async_copy(cnt.at[0], blocks, sems.at[8])
    count.start()

    def fill(colour_ref, normal_ref):
        copies = []
        for ch in range(4):
            at = rows(ch * TILE, TILE)
            colour, normal = (rad.at[0, ch], nor.at[0, ch]) if ch < 3 else (mom.at[0], dep.at[0])
            copies.append(pltpu.make_async_copy(colour, colour_ref.at[at, :], sems.at[ch]))
            copies.append(pltpu.make_async_copy(normal, normal_ref.at[at, :], sems.at[4 + ch]))
        for copy in copies:
            copy.start()
        for copy in copies:
            copy.wait()

    @pl.when(core == 0)
    def _():
        fill(keep, send)

    @pl.when(core == 1)
    def _():
        fill(send, keep)

    count.wait()
    number = blocks[...].astype(jnp.float32)
    for ref in (keep, send):
        ref[4 * TILE :, :] = jnp.zeros((8, TILE), jnp.float32)
        ref[4 * TILE :, 0:8] = number


def side_by_side(half_col, lane, left, right):
    return jnp.where(
        lane < HALF,
        jnp.where(half_col == 0, left, pltpu.roll(left, HALF, 1)),
        jnp.where(half_col == 0, pltpu.roll(right, HALF, 1), right),
    )


def pair_kernel(keep, recv, *outs):
    _, half_row, half_col, _, _ = place()
    lane = lax.broadcasted_iota(jnp.int32, (HALF, TILE), 1)
    flips = ((0, 0), (0, 1), (1, 1), (1, 0))
    counts = keep[4 * TILE :, :] + recv[4 * TILE :, :]
    for row in range(2):
        total = []
        for ch in range(4):
            at = rows(aligned(ch * TILE + HALF * (half_row if row == 0 else 1 - half_row)), HALF)
            total.append(keep[at, :] + recv[at, :])
        for k in range(4):
            if flips[k][0] == row:
                col = half_col if flips[k][1] == 0 else 1 - half_col
                for p in range(2):
                    outs[k][p * HALF : (p + 1) * HALF, :] = side_by_side(
                        col, lane, total[2 * p], total[2 * p + 1]
                    )
                outs[k][TILE:, :] = counts


def mean_kernel(own, r1, r2, r3, field, samples):
    core, half_row, half_col, _, _ = place()
    lane = lax.broadcasted_iota(jnp.int32, (8, TILE), 1)

    def total(at):
        return (own[at, :] + r1[at, :]) + (r2[at, :] + r3[at, :])

    blocks = total(rows(TILE, 8))
    spread = jnp.zeros((8, TILE), jnp.float32)
    for j in range(8):
        spread = jnp.where(lane // BLK == j, blocks[:, j : j + 1], spread)
    samples[...] = side_by_side(half_col, lane, spread, spread)
    wide = lax.broadcasted_iota(jnp.int32, (BLK, TILE), 1)
    for i in range(HALF // BLK):
        count = jnp.broadcast_to(samples[rows(4 * half_row + i, 1), :], (BLK, TILE))
        first, second = (total(rows(p * HALF + i * BLK, BLK)) / count for p in range(2))
        luma = luminance(first, pltpu.roll(first, HALF, 1), second)
        variance = jnp.maximum(second - jnp.square(pltpu.roll(luma, HALF, 1)), 0.0)
        second = jnp.where((core == 0) & (wide >= HALF), variance, second)
        field[rows(i * BLK, BLK), :] = first
        field[rows(HALF + i * BLK, BLK), :] = second


def in_order(core, mine, theirs):
    return (
        jnp.where(core == 0, mine[...], theirs[...]),
        jnp.where(core == 0, theirs[...], mine[...]),
    )


def column_kernel(mine, theirs, rim):
    core = place()[0]
    lane = lax.broadcasted_iota(jnp.int32, (HALF, TILE), 1)
    for g, field in enumerate(in_order(core, mine, theirs)):
        packed = jnp.zeros((HALF, TILE), jnp.float32)
        for ch in range(4):
            pair = field[(ch // 2) * HALF : (ch // 2 + 1) * HALF, :]
            by = TILE + 32 * ch - HALF * (ch % 2) - 32 * core
            packed = jnp.where(lane // 32 == ch, pltpu.roll(pair, lax.rem(by, TILE), 1), packed)
        rim[g * HALF : (g + 1) * HALF, :] = packed


def row_kernel(mine, theirs, side, other_side, window, rim):
    core, _, half_col, _, tx = place()
    lane = lax.broadcasted_iota(jnp.int32, (HALF, TILE), 1)
    is_left, is_right = lane < 32, lane >= 96
    outside = (is_left & (half_col == 0) & (tx == 0)) | (
        is_right & (half_col == 1) & (tx == lax.axis_size("tx") - 1)
    )
    left, right = in_order(core, side, other_side)
    for g, field in enumerate(in_order(core, mine, theirs)):
        lhs, rhs = (v[g * HALF : (g + 1) * HALF, :] for v in (left, right))
        for ch in range(4):
            pair = field[(ch // 2) * HALF : (ch // 2 + 1) * HALF, :]
            value = pltpu.roll(pair, 32 if ch % 2 == 0 else TILE - 32, 1)
            value = jnp.where(is_left, pltpu.roll(lhs, (TILE - 32 * ch) % TILE, 1), value)
            value = jnp.where(is_right, pltpu.roll(rhs, 96 - 32 * ch, 1), value)
            if g == 1 and ch == 3:
                value = jnp.where(outside, FAR, value * (1.0 / SIGMA_DEPTH))
            window[4 * g + ch] = value
    for f in range(8):
        rim[f] = window[f, rows(aligned(32 * core), RIM), :]


MOVES = (-16, -8, -4, -2, -1, 1, 2, 4, 8, 16)


def roll(value, by):
    return pltpu.roll(value, -by % TILE, 1)


def run_level(level, first, last, cur, geo, cur_moved, geo_moved, made, emit):
    dil = 2**level
    for r in range((first - 2 * dil) // 8 * 8, last + 2 * dil, 8):
        at = rows(r, 8)
        for b in (-2, -1, 1, 2):
            if (b * dil, r) not in made:
                made.add((b * dil, r))
                for f in range(4):
                    geo_moved[MOVES.index(b * dil), f, at, :] = roll(geo[f, at, :], b * dil)
            moved = [roll(cur[level, f, at, :], b * dil) for f in range(4)]
            moved.append(luminance(*moved[:3]))
            for f in range(5):
                cur_moved[level, b + 2, f, at, :] = moved[f]

    for r in range(first, last, 8):
        here = rows(r, 8)
        n0, n1, n2, depth = (geo[f, here, :] for f in range(4))
        luma = cur[level, 4, here, :]
        slope = -1.0 / (SIGMA_LUMA * jnp.sqrt(cur[level, 3, here, :]) + LUMA_FLOOR)
        sums = None
        for a in range(-2, 3):
            at = rows(r + a * dil, 8)
            for b in range(-2, 3):
                if b == 0:
                    g = [geo[f, at, :] for f in range(4)]
                    t = [cur[level, f, at, :] for f in range(5)]
                else:
                    g = [geo_moved[MOVES.index(b * dil), f, at, :] for f in range(4)]
                    t = [cur_moved[level, b + 2, f, at, :] for f in range(5)]
                e = jnp.abs(t[4] - luma) * slope - jnp.abs(g[3] - depth)
                e = e - jnp.square(g[0] - n0) - jnp.square(g[1] - n1)
                e = e - jnp.square(g[2] - n2)
                w = (TAPS[a + 2] * TAPS[b + 2]) * jnp.exp(e)
                parts = (w, w * t[0], w * t[1], w * t[2], w * w * t[3])
                sums = parts if sums is None else [p + q for p, q in zip(sums, parts)]
        inv = 1.0 / sums[0]
        emit(r, sums[1] * inv, sums[2] * inv, sums[3] * inv, sums[4] * (inv * inv))


def into(cur, level):
    def emit(r, c0, c1, c2, var):
        for f, value in enumerate((c0, c1, c2, var, luminance(c0, c1, c2))):
            cur[level, f, rows(r, 8), :] = value

    return emit


def place_rows(cur, geo, at, source):
    for f in range(4):
        cur[0, f, at, :] = source[f]
        geo[f, at, :] = source[4 + f]
    cur[0, 4, at, :] = luminance(source[0], source[1], source[2])


INNER = ((4, 60), (8, 56), (16, 48))
OUTER = (
    ((4, 36), (8, 40), (16, 48), (32, 64)),
    ((60, 92), (56, 88), (48, 80), (32, 64)),
)


def inner_kernel(body, near, middle, far, cur, geo, cur_moved, geo_moved):
    core = place()[0]
    place_rows(cur, geo, rows(0, HALF), body)
    made = set()
    for level, (first, last) in enumerate(INNER):
        run_level(
            level, first, last, cur, geo, cur_moved, geo_moved, made, into(cur, level + 1)
        )
    for f in range(5):
        near[f] = jnp.where(core == 0, cur[1, f, 4:12, :], cur[1, f, 52:60, :])
        middle[f] = jnp.where(core == 0, cur[2, f, 8:24, :], cur[2, f, 40:56, :])
        far[f] = cur[3, f, 16:48, :]


def outer_kernel(body, edge, near, middle, far, out, cur, geo, cur_moved, geo_moved):
    core, half_row, _, ty, _ = place()

    def work(this):
        outside = (half_row == this) & (ty == (lax.axis_size("ty") - 1 if this else 0))
        place_rows(cur, geo, rows(RIM * (1 - this), HALF), body)
        edge_at = rows(HALF * this, RIM)
        place_rows(cur, geo, edge_at, edge)
        geo[3, edge_at, :] = jnp.where(outside, FAR, edge[7])
        for f in range(5):
            cur[1, f, rows(52 if this else 36, 8), :] = near[f]
            cur[2, f, rows(40, 16), :] = middle[f]
            cur[3, f, rows(16 if this else 48, 32), :] = far[f]
        made = set()

        def finish(r, c0, c1, c2, var):
            lane = lax.broadcasted_iota(jnp.int32, (8, TILE), 1)
            for k, (p, q) in enumerate(((c0, c1), (c2, var))):
                out[rows(k * 32 + r - 32, 8), :] = jnp.where(lane < HALF, roll(p, 32), roll(q, -32))

        for level, (first, last) in enumerate(OUTER[this]):
            emit = into(cur, level + 1) if level < 3 else finish
            run_level(level, first, last, cur, geo, cur_moved, geo_moved, made, emit)

    for this in range(2):
        pl.when(core == this)(functools.partial(work, this))


def tile_kernel(*refs):
    ins, colour, variance = refs[:8], refs[8], refs[9]
    core, half_row, half_col, _, _ = place()
    lane = lax.broadcasted_iota(jnp.int32, (32, TILE), 1)
    low = lane < HALF
    for side in range(2):
        which = core if side == 0 else 1 - core
        for r in range(2):
            row = aligned(64 * (half_row if r == 0 else 1 - half_row) + 32 * which)
            near, other = (ins[side * 4 + k] for k in ((0, 1) if r == 0 else (3, 2)))
            for k in range(2):
                p, q = near[k * 32 : (k + 1) * 32, :], other[k * 32 : (k + 1) * 32, :]
                left = jnp.where(half_col == 0, p, q)
                right = jnp.where(half_col == 0, q, p)
                first = jnp.where(low, left, pltpu.roll(right, HALF, 1))
                second = jnp.where(low, pltpu.roll(left, HALF, 1), right)
                at = rows(row, 32)
                colour[2 * k, at, :] = first
                if k == 0:
                    colour[1, at, :] = second
                else:
                    variance[at, :] = second


def estimate(units, levels):
    taps = units * 25 * 8 * TILE
    return pl.CostEstimate(flops=27 * taps, transcendentals=taps, bytes_accessed=levels * 2**16)


def call(kernel, shapes, scratch=(), space=None, cost=None):
    return pl.pallas_call(
        kernel,
        **({"in_specs": [pl.BlockSpec(memory_space=pltpu.HBM)] * space} if space else {}),
        out_shape=[jax.ShapeDtypeStruct(s, jnp.float32) for s in shapes],
        scratch_shapes=list(scratch),
        **({"cost_estimate": estimate(*cost)} if cost else {}),
        compiler_params=pltpu.CompilerParams(vmem_limit_bytes=24 * 2**20),
    )


def run_filter(body, send_edge):
    edge = send_edge()

    def scratch(depth):
        return [
            pltpu.VMEM(shape, jnp.float32)
            for shape in (
                (4, 5, depth, TILE),
                (4, depth, TILE),
                (4, 5, 5, depth, TILE),
                (10, 4, depth, TILE),
            )
        ]

    inner = call(
        inner_kernel, [(5, 8, TILE), (5, 16, TILE), (5, 32, TILE)], scratch(HALF), cost=(17, 3)
    )(body)
    return call(outer_kernel, [(HALF, TILE)], scratch(WIN), cost=(16, 4))(body, edge, *inner)[0]


def pairs(sizes, partner):
    n_samp, n_ty, n_tx = sizes
    out = []
    for samp in range(n_samp):
        for ty in range(n_ty):
            for tx in range(n_tx):
                to = partner(samp, ty, tx)
                if 0 <= to[1] < n_ty and 0 <= to[2] < n_tx:
                    out.append(
                        ((samp * n_ty + ty) * n_tx + tx, (to[0] * n_ty + to[1]) * n_tx + to[2])
                    )
    return out


def beside(samp, ty, tx):
    y, core = samp // 2, samp % 2
    half_col = ((y + 1) % 4 // 2 + tx) % 2
    if half_col == core:
        return samp ^ 1, ty, tx + (1 if core else -1)
    return samp ^ 3, ty, tx


def above(samp, ty, tx):
    y, core = samp // 2, samp % 2
    half_row = (y // 2 + ty) % 2
    if half_row == core:
        return samp ^ 1, ty + (1 if core else -1), tx
    return samp ^ 7, ty, tx


def per_device(sizes, radiance, moment, normal, depth_sum, counts):
    def send(value, partner):
        return lax.ppermute(value, AXES, pairs(sizes, partner))

    def other_core(value):
        return send(value, lambda s, ty, tx: (s ^ 1, ty, tx))

    def other_y(value, k):
        return send(value, lambda s, ty, tx: (s ^ (2 * k), ty, tx))

    packed = (4 * TILE + 8, TILE)
    keep, give = call(
        pack_kernel,
        [packed, packed],
        [pltpu.VMEM((8, 8), jnp.int32), pltpu.SemaphoreType.DMA((9,))],
        5,
    )(
        *(
            pltpu.with_memory_space_constraint(value, pltpu.HBM)
            for value in (radiance, moment, normal, depth_sum, counts)
        )
    )
    quarter = (TILE + 8, TILE)
    parts = list(call(pair_kernel, [quarter] * 4)(keep, other_core(give)))
    parts = parts[:1] + [other_y(parts[k], k) for k in (1, 2, 3)]
    (mine,) = call(mean_kernel, [(TILE, TILE)], [pltpu.VMEM((8, TILE), jnp.float32)])(*parts)
    theirs = other_core(mine)
    (rim,) = call(column_kernel, [(TILE, TILE)])(mine, theirs)
    rim = send(rim, beside)
    body, edge = call(row_kernel, [(8, HALF, TILE), (8, RIM, TILE)])(
        mine, theirs, rim, other_core(rim)
    )
    done = run_filter(body, lambda: send(edge, above))
    got = [done] + [other_y(done, k) for k in (1, 2, 3)]
    theirs = [other_core(g) for g in got]
    return tuple(call(tile_kernel, [(3, TILE, TILE), (TILE, TILE)])(*got, *theirs))


def solution(mesh):
    sizes = tuple(mesh.shape[axis] for axis in AXES)
    placed = (
        P("samp", None, "ty", "tx"),
        P("samp", "ty", "tx"),
        P("samp", None, "ty", "tx"),
        P("samp", "ty", "tx"),
        P("samp", "ty", "tx"),
    )
    return jax.shard_map(
        functools.partial(per_device, sizes),
        mesh=mesh,
        in_specs=placed,
        out_specs=(P(None, "ty", "tx"), P("ty", "tx")),
        check_vma=False,
    )
```

```python
import functools

import jax
import jax.numpy as jnp
from jax import lax
from jax.experimental import pallas as pl
from jax.experimental.pallas import tpu as pltpu
from jax.sharding import PartitionSpec as P

TAPS = (0.0625, 0.25, 0.375, 0.25, 0.0625)
LUMA = (0.2126, 0.7152, 0.0722)
SIGMA_DEPTH = 0.5
SIGMA_NORMAL = 1.0
SIGMA_LUMA = 4.0
LUMA_FLOOR = 0.5
FAR = 1e30

TILE = 128
HALF = 64
RIM = 32
WIN = 96
BLK = 16
AXES = ("samp", "ty", "tx")


def place():
    samp = lax.axis_index("samp")
    ty = lax.axis_index("ty")
    tx = lax.axis_index("tx")
    core = lax.rem(samp, 2)
    y = samp // 2
    half_row = lax.rem(y // 2 + ty, 2)
    half_col = lax.rem(lax.rem(y + 1, 4) // 2 + tx, 2)
    return core, half_row, half_col, ty, tx


def edge_of(core, half_row):
    return lax.rem(core + half_row, 2)


def luminance(c0, c1, c2):
    return LUMA[0] * c0 + LUMA[1] * c1 + LUMA[2] * c2


def rows(start, count):
    return pl.ds(start, count)


def aligned(value):
    return pl.multiple_of(value, 8)


def pick_kernel(wanted, rad, mom, nor, dep, cnt, picked, blocks, sems):
    core = place()[0]
    count = pltpu.make_async_copy(cnt.at[0], blocks, sems.at[4])
    count.start()

    def fill(first, last):
        copies = []
        for ch in range(4):
            source = first.at[0, ch] if ch < 3 else last.at[0]
            copies.append(
                pltpu.make_async_copy(source, picked.at[rows(ch * TILE, TILE), :], sems.at[ch])
            )
        for copy in copies:
            copy.start()
        for copy in copies:
            copy.wait()

    @pl.when(core == wanted)
    def _():
        fill(rad, mom)

    @pl.when(core != wanted)
    def _():
        fill(nor, dep)

    count.wait()
    picked[4 * TILE :, :] = jnp.zeros((8, TILE), jnp.float32)
    picked[4 * TILE :, 0:8] = blocks[...].astype(jnp.float32)


def pair_kernel(keep, recv, *outs):
    _, half_row, half_col, _, _ = place()
    lane = lax.broadcasted_iota(jnp.int32, (HALF, TILE), 1)
    flips = ((0, 0), (0, 1), (1, 1), (1, 0))
    counts = keep[4 * TILE :, :] + recv[4 * TILE :, :]
    for row in range(2):
        total = []
        for ch in range(4):
            at = rows(aligned(ch * TILE + HALF * (half_row if row == 0 else 1 - half_row)), HALF)
            total.append(keep[at, :] + recv[at, :])
        moved = [pltpu.roll(total[3], 96 - 32 * p, 1) for p in range(3)]
        for k in range(4):
            if flips[k][0] == row:
                col = half_col if flips[k][1] == 0 else 1 - half_col
                free = lane // 32 == 3 - 3 * col
                for p in range(3):
                    outs[k][p * HALF : (p + 1) * HALF, :] = jnp.where(free, moved[p], total[p])
                outs[k][3 * HALF :, :] = counts


def mean_kernel(own, r1, r2, r3, field, rim, samples):
    core, half_row, half_col, _, _ = place()
    lane = lax.broadcasted_iota(jnp.int32, (8, TILE), 1)

    def total(at):
        return (own[at, :] + r1[at, :]) + (r2[at, :] + r3[at, :])

    blocks = total(rows(3 * HALF, 8))
    spread = jnp.zeros((8, TILE), jnp.float32)
    for j in range(8):
        spread = jnp.where(lane // BLK == j, blocks[:, j : j + 1], spread)
    samples[...] = spread
    group = lax.broadcasted_iota(jnp.int32, (BLK, TILE), 1) // 32
    for i in range(HALF // BLK):
        count = jnp.broadcast_to(samples[rows(4 * half_row + i, 1), :], (BLK, TILE))
        sums = [total(rows(p * HALF + i * BLK, BLK)) for p in range(3)]
        last = sums[0]
        for p in range(3):
            last = jnp.where(group == p + half_col, pltpu.roll(sums[p], 32 * p + 32, 1), last)
        mean = [value / count for value in (*sums, last)]
        variance = jnp.maximum(mean[3] - jnp.square(luminance(*mean[:3])), 0.0)
        mean[3] = jnp.where(core == 0, variance, mean[3])
        packed = jnp.zeros((BLK, TILE), jnp.float32)
        for ch in range(4):
            field[rows(ch * HALF + i * BLK, BLK), :] = mean[ch]
            moved = pltpu.roll(mean[ch], lax.rem(32 * ch + 32 * half_col, TILE), 1)
            packed = jnp.where(group == ch, moved, packed)
        rim[rows(i * BLK, BLK), :] = packed


def in_order(core, mine, theirs):
    return (
        jnp.where(core == 0, mine[...], theirs[...]),
        jnp.where(core == 0, theirs[...], mine[...]),
    )


def row_kernel(mine, theirs, side, other_side, window, edge):
    core, half_row, half_col, _, tx = place()
    first = aligned(32 * edge_of(core, half_row))
    lane = lax.broadcasted_iota(jnp.int32, (HALF, TILE), 1)
    rim_lane = lane // 32 == 3 * half_col
    outside = rim_lane & (tx == half_col * (lax.axis_size("tx") - 1))
    rims = in_order(core, side, other_side)
    for g, field in enumerate(in_order(core, mine, theirs)):
        for ch in range(4):
            value = pltpu.roll(field[ch * HALF : (ch + 1) * HALF, :], 32 + 64 * half_col, 1)
            rim = pltpu.roll(rims[g], lax.rem(TILE - 32 * ch + 96 * half_col, TILE), 1)
            value = jnp.where(rim_lane, rim, value)
            if g == 1 and ch == 3:
                value = jnp.where(outside, FAR, value * (1.0 / SIGMA_DEPTH))
            window[4 * g + ch] = value
    for f in range(8):
        edge[f] = window[f, rows(first, RIM), :]


MOVES = (-16, -8, -4, -2, -1, 1, 2, 4, 8, 16)


def roll(value, by):
    return pltpu.roll(value, -by % TILE, 1)


def run_level(level, first, last, cur, geo, cur_moved, geo_moved, made, emit):
    dil = 2**level
    for r in range((first - 2 * dil) // 8 * 8, last + 2 * dil, 8):
        at = rows(r, 8)
        for b in (-2, -1, 1, 2):
            if (b * dil, r) not in made:
                made.add((b * dil, r))
                for f in range(4):
                    geo_moved[MOVES.index(b * dil), f, at, :] = roll(geo[f, at, :], b * dil)
            moved = [roll(cur[level, f, at, :], b * dil) for f in range(4)]
            moved.append(luminance(*moved[:3]))
            for f in range(5):
                cur_moved[level, b + 2, f, at, :] = moved[f]

    for r in range(first, last, 8):
        here = rows(r, 8)
        n0, n1, n2, depth = (geo[f, here, :] for f in range(4))
        luma = cur[level, 4, here, :]
        slope = -1.0 / (SIGMA_LUMA * jnp.sqrt(cur[level, 3, here, :]) + LUMA_FLOOR)
        sums = None
        for a in range(-2, 3):
            at = rows(r + a * dil, 8)
            for b in range(-2, 3):
                if b == 0:
                    g = [geo[f, at, :] for f in range(4)]
                    t = [cur[level, f, at, :] for f in range(5)]
                else:
                    g = [geo_moved[MOVES.index(b * dil), f, at, :] for f in range(4)]
                    t = [cur_moved[level, b + 2, f, at, :] for f in range(5)]
                e = jnp.abs(t[4] - luma) * slope - jnp.abs(g[3] - depth)
                e = e - jnp.square(g[0] - n0) - jnp.square(g[1] - n1)
                e = e - jnp.square(g[2] - n2)
                w = (TAPS[a + 2] * TAPS[b + 2]) * jnp.exp(e)
                parts = (w, w * t[0], w * t[1], w * t[2], w * w * t[3])
                sums = parts if sums is None else [p + q for p, q in zip(sums, parts)]
        inv = 1.0 / sums[0]
        emit(r, sums[1] * inv, sums[2] * inv, sums[3] * inv, sums[4] * (inv * inv))


def into(cur, level):
    def emit(r, c0, c1, c2, var):
        for f, value in enumerate((c0, c1, c2, var, luminance(c0, c1, c2))):
            cur[level, f, rows(r, 8), :] = value

    return emit


def place_rows(cur, geo, at, source):
    for f in range(4):
        cur[0, f, at, :] = source[f]
        geo[f, at, :] = source[4 + f]
    cur[0, 4, at, :] = luminance(source[0], source[1], source[2])


INNER = ((4, 60), (8, 56), (16, 48))
OUTER = (
    ((4, 36), (8, 40), (16, 48), (32, 64)),
    ((60, 92), (56, 88), (48, 80), (32, 64)),
)


def inner_kernel(body, near, middle, far, cur, geo, cur_moved, geo_moved):
    core, half_row, _, _, _ = place()
    upper = edge_of(core, half_row) == 0
    place_rows(cur, geo, rows(0, HALF), body)
    made = set()
    for level, (first, last) in enumerate(INNER):
        run_level(
            level, first, last, cur, geo, cur_moved, geo_moved, made, into(cur, level + 1)
        )
    for f in range(5):
        near[f] = jnp.where(upper, cur[1, f, 4:12, :], cur[1, f, 52:60, :])
        middle[f] = jnp.where(upper, cur[2, f, 8:24, :], cur[2, f, 40:56, :])
        far[f] = cur[3, f, 16:48, :]


def outer_kernel(body, edge, near, middle, far, out, cur, geo, cur_moved, geo_moved):
    core, half_row, _, ty, _ = place()

    def work(this):
        outside = (half_row == this) & (ty == (lax.axis_size("ty") - 1 if this else 0))
        place_rows(cur, geo, rows(RIM * (1 - this), HALF), body)
        edge_at = rows(HALF * this, RIM)
        place_rows(cur, geo, edge_at, edge)
        geo[3, edge_at, :] = jnp.where(outside, FAR, edge[7])
        for f in range(5):
            cur[1, f, rows(52 if this else 36, 8), :] = near[f]
            cur[2, f, rows(40, 16), :] = middle[f]
            cur[3, f, rows(16 if this else 48, 32), :] = far[f]
        made = set()

        def finish(r, c0, c1, c2, var):
            lane = lax.broadcasted_iota(jnp.int32, (8, TILE), 1)
            for k, (p, q) in enumerate(((c0, c1), (c2, var))):
                out[rows(k * 32 + r - 32, 8), :] = jnp.where(lane < HALF, roll(p, 32), roll(q, -32))

        for level, (first, last) in enumerate(OUTER[this]):
            emit = into(cur, level + 1) if level < 3 else finish
            run_level(level, first, last, cur, geo, cur_moved, geo_moved, made, emit)

    for this in range(2):
        pl.when(edge_of(core, half_row) == this)(functools.partial(work, this))


def tile_kernel(*refs):
    ins, colour, variance = refs[:8], refs[8], refs[9]
    core, half_row, half_col, _, _ = place()
    lane = lax.broadcasted_iota(jnp.int32, (32, TILE), 1)
    low = lane < HALF
    for side in range(2):
        which = core if side == 0 else 1 - core
        for r in range(2):
            half = half_row if r == 0 else 1 - half_row
            row = aligned(64 * half + 32 * edge_of(which, half))
            near, other = (ins[side * 4 + k] for k in ((0, 1) if r == 0 else (3, 2)))
            for k in range(2):
                p, q = near[k * 32 : (k + 1) * 32, :], other[k * 32 : (k + 1) * 32, :]
                left = jnp.where(half_col == 0, p, q)
                right = jnp.where(half_col == 0, q, p)
                first = jnp.where(low, left, pltpu.roll(right, HALF, 1))
                second = jnp.where(low, pltpu.roll(left, HALF, 1), right)
                at = rows(row, 32)
                colour[2 * k, at, :] = first
                if k == 0:
                    colour[1, at, :] = second
                else:
                    variance[at, :] = second


def estimate(units, levels):
    taps = units * 25 * 8 * TILE
    return pl.CostEstimate(flops=27 * taps, transcendentals=taps, bytes_accessed=levels * 2**16)


def call(kernel, shapes, scratch=(), space=None, cost=None):
    return pl.pallas_call(
        kernel,
        **({"in_specs": [pl.BlockSpec(memory_space=pltpu.HBM)] * space} if space else {}),
        out_shape=[jax.ShapeDtypeStruct(s, jnp.float32) for s in shapes],
        scratch_shapes=list(scratch),
        **({"cost_estimate": estimate(*cost)} if cost else {}),
        compiler_params=pltpu.CompilerParams(vmem_limit_bytes=24 * 2**20),
    )


def run_filter(body, send_edge):
    edge = send_edge()

    def scratch(depth):
        return [
            pltpu.VMEM(shape, jnp.float32)
            for shape in (
                (4, 5, depth, TILE),
                (4, depth, TILE),
                (4, 5, 5, depth, TILE),
                (10, 4, depth, TILE),
            )
        ]

    inner = call(
        inner_kernel, [(5, 8, TILE), (5, 16, TILE), (5, 32, TILE)], scratch(HALF), cost=(17, 3)
    )(body)
    return call(outer_kernel, [(HALF, TILE)], scratch(WIN), cost=(16, 4))(body, edge, *inner)[0]


def pairs(sizes, partner, spare=0):
    n_samp, n_ty, n_tx = sizes

    def flat(samp, ty, tx):
        return (samp * n_ty + ty) * n_tx + tx

    out = []
    for samp in range(n_samp):
        for ty in range(n_ty):
            for tx in range(n_tx):
                to = partner(samp, ty, tx)
                if not (0 <= to[1] < n_ty and 0 <= to[2] < n_tx):
                    to = samp ^ spare, ty, tx
                out.append((flat(samp, ty, tx), flat(*to)))
    return out


def across(samp, ty, tx):
    half_col = ((samp // 2 + 1) % 4 // 2 + tx) % 2
    return samp, ty, tx + (1 if half_col else -1)


def beyond(samp, ty, tx):
    if samp % 2:
        return samp ^ 6, ty, tx
    return samp, ty + (1 if (samp // 4 + ty) % 2 else -1), tx


def per_device(sizes, radiance, moment, normal, depth_sum, counts):
    def send(value, partner, spare=0):
        return lax.ppermute(value, AXES, pairs(sizes, partner, spare))

    def other_core(value):
        return send(value, lambda s, ty, tx: (s ^ 1, ty, tx))

    def other_y(value, k):
        return send(value, lambda s, ty, tx: (s ^ (2 * k), ty, tx))

    packed = (4 * TILE + 8, TILE)
    inputs = [
        pltpu.with_memory_space_constraint(value, pltpu.HBM)
        for value in (radiance, moment, normal, depth_sum, counts)
    ]

    def pick(wanted):
        return call(
            functools.partial(pick_kernel, wanted),
            [packed],
            [pltpu.VMEM((8, 8), jnp.int32), pltpu.SemaphoreType.DMA((5,))],
            5,
            (1, 4),
        )(*inputs)[0]

    give = pick(1)
    keep = pick(0)
    part = (3 * HALF + 8, TILE)
    parts = list(call(pair_kernel, [part] * 4)(keep, other_core(give)))
    parts = parts[:1] + [other_y(parts[k], k) for k in (1, 2, 3)]
    mine, rim = call(
        mean_kernel, [(4 * HALF, TILE), (HALF, TILE)], [pltpu.VMEM((8, TILE), jnp.float32)]
    )(*parts)
    rim = send(rim, across, 6)
    body, edge = call(row_kernel, [(8, HALF, TILE), (8, RIM, TILE)])(
        mine, other_core(mine), rim, other_core(rim)
    )
    done = run_filter(body, lambda: send(edge, beyond, 2))
    got = [done] + [other_y(done, k) for k in (1, 2, 3)]
    theirs = [other_core(g) for g in got]
    return tuple(call(tile_kernel, [(3, TILE, TILE), (TILE, TILE)])(*got, *theirs))


def solution(mesh):
    sizes = tuple(mesh.shape[axis] for axis in AXES)
    placed = (
        P("samp", None, "ty", "tx"),
        P("samp", "ty", "tx"),
        P("samp", None, "ty", "tx"),
        P("samp", "ty", "tx"),
        P("samp", "ty", "tx"),
    )
    return jax.shard_map(
        functools.partial(per_device, sizes),
        mesh=mesh,
        in_specs=placed,
        out_specs=(P(None, "ty", "tx"), P("ty", "tx")),
        check_vma=False,
    )
```

```python
import functools

import jax
import jax.numpy as jnp
from jax import lax
from jax.experimental import pallas as pl
from jax.experimental.pallas import tpu as pltpu
from jax.sharding import PartitionSpec as P

TAPS = (0.0625, 0.25, 0.375, 0.25, 0.0625)
LUMA = (0.2126, 0.7152, 0.0722)
SIGMA_DEPTH = 0.5
SIGMA_NORMAL = 1.0
SIGMA_LUMA = 4.0
LUMA_FLOOR = 0.5
FAR = 1e30

TILE = 128
HALF = 64
RIM = 32
WIN = 96
BLK = 16
AXES = ("samp", "ty", "tx")


def place():
    samp = lax.axis_index("samp")
    ty = lax.axis_index("ty")
    tx = lax.axis_index("tx")
    core = lax.rem(samp, 2)
    y = samp // 2
    half_row = lax.rem(y // 2 + ty, 2)
    half_col = lax.rem(lax.rem(y + 1, 4) // 2 + tx, 2)
    return core, half_row, half_col, ty, tx


def edge_of(core, half_row):
    return lax.rem(core + half_row, 2)


def luminance(c0, c1, c2):
    return LUMA[0] * c0 + LUMA[1] * c1 + LUMA[2] * c2


def rows(start, count):
    return pl.ds(start, count)


def aligned(value):
    return pl.multiple_of(value, 8)


def pick_kernel(wanted, rad, mom, nor, dep, cnt, picked, blocks, sems):
    core = place()[0]
    count = pltpu.make_async_copy(cnt.at[0], blocks, sems.at[4])
    count.start()

    def fill(first, last):
        copies = []
        for ch in range(4):
            source = first.at[0, ch] if ch < 3 else last.at[0]
            copies.append(
                pltpu.make_async_copy(source, picked.at[rows(ch * TILE, TILE), :], sems.at[ch])
            )
        for copy in copies:
            copy.start()
        for copy in copies:
            copy.wait()

    @pl.when(core == wanted)
    def _():
        fill(rad, mom)

    @pl.when(core != wanted)
    def _():
        fill(nor, dep)

    count.wait()
    picked[4 * TILE :, :] = jnp.zeros((8, TILE), jnp.float32)
    picked[4 * TILE :, 0:8] = blocks[...].astype(jnp.float32)


def pair_kernel(keep, recv, *outs):
    _, half_row, half_col, _, _ = place()
    lane = lax.broadcasted_iota(jnp.int32, (HALF, TILE), 1)
    flips = ((0, 0), (0, 1), (1, 1), (1, 0))
    counts = keep[4 * TILE :, :] + recv[4 * TILE :, :]
    for row in range(2):
        total = []
        for ch in range(4):
            at = rows(aligned(ch * TILE + HALF * (half_row if row == 0 else 1 - half_row)), HALF)
            total.append(keep[at, :] + recv[at, :])
        moved = [pltpu.roll(total[3], 96 - 32 * p, 1) for p in range(3)]
        for k in range(4):
            if flips[k][0] == row:
                col = half_col if flips[k][1] == 0 else 1 - half_col
                free = lane // 32 == 3 - 3 * col
                for p in range(3):
                    outs[k][p * HALF : (p + 1) * HALF, :] = jnp.where(free, moved[p], total[p])
                outs[k][3 * HALF :, :] = counts


def mean_kernel(wants_rim, own, r1, r2, r3, out, samples):
    core, half_row, half_col, _, _ = place()
    lane = lax.broadcasted_iota(jnp.int32, (8, TILE), 1)

    def total(at):
        return (own[at, :] + r1[at, :]) + (r2[at, :] + r3[at, :])

    blocks = total(rows(3 * HALF, 8))
    spread = jnp.zeros((8, TILE), jnp.float32)
    for j in range(8):
        spread = jnp.where(lane // BLK == j, blocks[:, j : j + 1], spread)
    samples[...] = spread
    group = lax.broadcasted_iota(jnp.int32, (BLK, TILE), 1) // 32
    for i in range(HALF // BLK):
        count = jnp.broadcast_to(samples[rows(4 * half_row + i, 1), :], (BLK, TILE))
        sums = [total(rows(p * HALF + i * BLK, BLK)) for p in range(3)]
        last = sums[0]
        for p in range(3):
            last = jnp.where(group == p + half_col, pltpu.roll(sums[p], 32 * p + 32, 1), last)
        mean = [value / count for value in (*sums, last)]
        variance = jnp.maximum(mean[3] - jnp.square(luminance(*mean[:3])), 0.0)
        mean[3] = jnp.where(core == 0, variance, mean[3])
        packed = jnp.zeros((BLK, TILE), jnp.float32)
        for ch in range(4):
            if wants_rim:
                moved = pltpu.roll(mean[ch], lax.rem(32 * ch + 32 * half_col, TILE), 1)
                packed = jnp.where(group == ch, moved, packed)
            else:
                out[rows(ch * HALF + i * BLK, BLK), :] = mean[ch]
        if wants_rim:
            out[rows(i * BLK, BLK), :] = packed


def row_kernel(wants_edge, mine, theirs, side, other_side, out):
    core, half_row, half_col, _, tx = place()
    count = RIM if wants_edge else HALF
    first = aligned(32 * edge_of(core, half_row)) if wants_edge else 0
    rim_lane = lax.broadcasted_iota(jnp.int32, (count, TILE), 1) // 32 == 3 * half_col
    outside = rim_lane & (tx == half_col * (lax.axis_size("tx") - 1))

    def fill(colour, normal, colour_rim, normal_rim):
        for g, (field, rims) in enumerate(((colour, colour_rim), (normal, normal_rim))):
            for ch in range(4):
                at = ch * HALF + first
                value = field[rows(aligned(at) if wants_edge else at, count), :]
                value = pltpu.roll(value, 32 + 64 * half_col, 1)
                by = lax.rem(TILE - 32 * ch + 96 * half_col, TILE)
                value = jnp.where(rim_lane, pltpu.roll(rims[rows(first, count), :], by, 1), value)
                if g == 1 and ch == 3:
                    value = jnp.where(outside, FAR, value * (1.0 / SIGMA_DEPTH))
                out[4 * g + ch] = value

    @pl.when(core == 0)
    def _():
        fill(mine, theirs, side, other_side)

    @pl.when(core == 1)
    def _():
        fill(theirs, mine, other_side, side)


MOVES = (-16, -8, -4, -2, -1, 1, 2, 4, 8, 16)


def roll(value, by):
    return pltpu.roll(value, -by % TILE, 1)


def run_level(level, first, last, cur, geo, cur_moved, geo_moved, made, emit):
    dil = 2**level
    for r in range((first - 2 * dil) // 8 * 8, last + 2 * dil, 8):
        at = rows(r, 8)
        for b in (-2, -1, 1, 2):
            if (b * dil, r) not in made:
                made.add((b * dil, r))
                for f in range(4):
                    geo_moved[MOVES.index(b * dil), f, at, :] = roll(geo[f, at, :], b * dil)
            moved = [roll(cur[level, f, at, :], b * dil) for f in range(4)]
            moved.append(luminance(*moved[:3]))
            for f in range(5):
                cur_moved[level, b + 2, f, at, :] = moved[f]

    for r in range(first, last, 8):
        here = rows(r, 8)
        n0, n1, n2, depth = (geo[f, here, :] for f in range(4))
        luma = cur[level, 4, here, :]
        slope = -1.0 / (SIGMA_LUMA * jnp.sqrt(cur[level, 3, here, :]) + LUMA_FLOOR)
        sums = None
        for a in range(-2, 3):
            at = rows(r + a * dil, 8)
            for b in range(-2, 3):
                if b == 0:
                    g = [geo[f, at, :] for f in range(4)]
                    t = [cur[level, f, at, :] for f in range(5)]
                else:
                    g = [geo_moved[MOVES.index(b * dil), f, at, :] for f in range(4)]
                    t = [cur_moved[level, b + 2, f, at, :] for f in range(5)]
                e = jnp.abs(t[4] - luma) * slope - jnp.abs(g[3] - depth)
                e = e - jnp.square(g[0] - n0) - jnp.square(g[1] - n1)
                e = e - jnp.square(g[2] - n2)
                w = (TAPS[a + 2] * TAPS[b + 2]) * jnp.exp(e)
                parts = (w, w * t[0], w * t[1], w * t[2], w * w * t[3])
                sums = parts if sums is None else [p + q for p, q in zip(sums, parts)]
        inv = 1.0 / sums[0]
        emit(r, sums[1] * inv, sums[2] * inv, sums[3] * inv, sums[4] * (inv * inv))


def into(cur, level):
    def emit(r, c0, c1, c2, var):
        for f, value in enumerate((c0, c1, c2, var, luminance(c0, c1, c2))):
            cur[level, f, rows(r, 8), :] = value

    return emit


def place_rows(cur, geo, at, source):
    for f in range(4):
        cur[0, f, at, :] = source[f]
        geo[f, at, :] = source[4 + f]
    cur[0, 4, at, :] = luminance(source[0], source[1], source[2])


INNER = ((4, 60), (8, 56), (16, 48))
OUTER = (
    ((4, 36), (8, 40), (16, 48), (32, 64)),
    ((60, 92), (56, 88), (48, 80), (32, 64)),
)


def inner_kernel(body, near, middle, far, cur, geo, cur_moved, geo_moved):
    core, half_row, _, _, _ = place()
    upper = edge_of(core, half_row) == 0
    place_rows(cur, geo, rows(0, HALF), body)
    made = set()
    for level, (first, last) in enumerate(INNER):
        run_level(
            level, first, last, cur, geo, cur_moved, geo_moved, made, into(cur, level + 1)
        )
    for f in range(5):
        near[f] = jnp.where(upper, cur[1, f, 4:12, :], cur[1, f, 52:60, :])
        middle[f] = jnp.where(upper, cur[2, f, 8:24, :], cur[2, f, 40:56, :])
        far[f] = cur[3, f, 16:48, :]


def outer_kernel(body, edge, near, middle, far, out, cur, geo, cur_moved, geo_moved):
    core, half_row, _, ty, _ = place()

    def work(this):
        outside = (half_row == this) & (ty == (lax.axis_size("ty") - 1 if this else 0))
        place_rows(cur, geo, rows(RIM * (1 - this), HALF), body)
        edge_at = rows(HALF * this, RIM)
        place_rows(cur, geo, edge_at, edge)
        geo[3, edge_at, :] = jnp.where(outside, FAR, edge[7])
        for f in range(5):
            cur[1, f, rows(52 if this else 36, 8), :] = near[f]
            cur[2, f, rows(40, 16), :] = middle[f]
            cur[3, f, rows(16 if this else 48, 32), :] = far[f]
        made = set()

        def finish(r, c0, c1, c2, var):
            lane = lax.broadcasted_iota(jnp.int32, (8, TILE), 1)
            for k, (p, q) in enumerate(((c0, c1), (c2, var))):
                out[rows(k * 32 + r - 32, 8), :] = jnp.where(lane < HALF, roll(p, 32), roll(q, -32))

        for level, (first, last) in enumerate(OUTER[this]):
            emit = into(cur, level + 1) if level < 3 else finish
            run_level(level, first, last, cur, geo, cur_moved, geo_moved, made, emit)

    for this in range(2):
        pl.when(edge_of(core, half_row) == this)(functools.partial(work, this))


def tile_kernel(*refs):
    ins, colour, variance = refs[:8], refs[8], refs[9]
    core, half_row, half_col, _, _ = place()
    lane = lax.broadcasted_iota(jnp.int32, (32, TILE), 1)
    low = lane < HALF
    for side in range(2):
        which = core if side == 0 else 1 - core
        for r in range(2):
            half = half_row if r == 0 else 1 - half_row
            row = aligned(64 * half + 32 * edge_of(which, half))
            near, other = (ins[side * 4 + k] for k in ((0, 1) if r == 0 else (3, 2)))
            for k in range(2):
                p, q = near[k * 32 : (k + 1) * 32, :], other[k * 32 : (k + 1) * 32, :]
                left = jnp.where(half_col == 0, p, q)
                right = jnp.where(half_col == 0, q, p)
                first = jnp.where(low, left, pltpu.roll(right, HALF, 1))
                second = jnp.where(low, pltpu.roll(left, HALF, 1), right)
                at = rows(row, 32)
                colour[2 * k, at, :] = first
                if k == 0:
                    colour[1, at, :] = second
                else:
                    variance[at, :] = second


def estimate(units, levels):
    taps = units * 25 * 8 * TILE
    return pl.CostEstimate(flops=27 * taps, transcendentals=taps, bytes_accessed=levels * 2**16)


def call(kernel, shapes, scratch=(), space=None, cost=None):
    return pl.pallas_call(
        kernel,
        **({"in_specs": [pl.BlockSpec(memory_space=pltpu.HBM)] * space} if space else {}),
        out_shape=[jax.ShapeDtypeStruct(s, jnp.float32) for s in shapes],
        scratch_shapes=list(scratch),
        **({"cost_estimate": estimate(*cost)} if cost else {}),
        compiler_params=pltpu.CompilerParams(vmem_limit_bytes=24 * 2**20),
    )


def run_filter(body, send_edge):
    edge = send_edge()

    def scratch(depth):
        return [
            pltpu.VMEM(shape, jnp.float32)
            for shape in (
                (4, 5, depth, TILE),
                (4, depth, TILE),
                (4, 5, 5, depth, TILE),
                (10, 4, depth, TILE),
            )
        ]

    inner = call(
        inner_kernel, [(5, 8, TILE), (5, 16, TILE), (5, 32, TILE)], scratch(HALF), cost=(17, 3)
    )(body)
    return call(outer_kernel, [(HALF, TILE)], scratch(WIN), cost=(16, 4))(body, edge, *inner)[0]


def pairs(sizes, partner, spare=0):
    n_samp, n_ty, n_tx = sizes

    def flat(samp, ty, tx):
        return (samp * n_ty + ty) * n_tx + tx

    out = []
    for samp in range(n_samp):
        for ty in range(n_ty):
            for tx in range(n_tx):
                to = partner(samp, ty, tx)
                if not (0 <= to[1] < n_ty and 0 <= to[2] < n_tx):
                    to = samp ^ spare, ty, tx
                out.append((flat(samp, ty, tx), flat(*to)))
    return out


def across(samp, ty, tx):
    half_col = ((samp // 2 + 1) % 4 // 2 + tx) % 2
    return samp, ty, tx + (1 if half_col else -1)


def beyond(samp, ty, tx):
    if samp % 2:
        return samp ^ 6, ty, tx
    return samp, ty + (1 if (samp // 4 + ty) % 2 else -1), tx


def per_device(sizes, radiance, moment, normal, depth_sum, counts):
    def send(value, partner, spare=0):
        return lax.ppermute(value, AXES, pairs(sizes, partner, spare))

    def other_core(value):
        return send(value, lambda s, ty, tx: (s ^ 1, ty, tx))

    def other_y(value, k):
        return send(value, lambda s, ty, tx: (s ^ (2 * k), ty, tx))

    packed = (4 * TILE + 8, TILE)
    inputs = [
        pltpu.with_memory_space_constraint(value, pltpu.HBM)
        for value in (radiance, moment, normal, depth_sum, counts)
    ]

    def pick(wanted):
        return call(
            functools.partial(pick_kernel, wanted),
            [packed],
            [pltpu.VMEM((8, 8), jnp.int32), pltpu.SemaphoreType.DMA((5,))],
            5,
            (1, 4),
        )(*inputs)[0]

    give = pick(1)
    keep = pick(0)
    part = (3 * HALF + 8, TILE)
    parts = list(call(pair_kernel, [part] * 4)(keep, other_core(give)))
    parts = parts[:1] + [other_y(parts[k], k) for k in (1, 2, 3)]

    def means(wants_rim):
        return call(
            functools.partial(mean_kernel, wants_rim),
            [(HALF if wants_rim else 4 * HALF, TILE)],
            [pltpu.VMEM((8, TILE), jnp.float32)],
            cost=(1, 4),
        )(*parts)[0]

    rim = send(means(True), across, 6)
    mine, rim = lax.optimization_barrier((means(False), rim))
    sides = (mine, other_core(mine), rim, other_core(rim))

    def joined(wants_edge, count):
        kernel = functools.partial(row_kernel, wants_edge)
        return call(kernel, [(8, count, TILE)], cost=(1, 8))(*sides)[0]

    edge = send(joined(True, RIM), beyond, 2)
    done = run_filter(joined(False, HALF), lambda: edge)
    got = [done] + [other_y(done, k) for k in (1, 2, 3)]
    theirs = [other_core(g) for g in got]
    return tuple(call(tile_kernel, [(3, TILE, TILE), (TILE, TILE)])(*got, *theirs))


def solution(mesh):
    sizes = tuple(mesh.shape[axis] for axis in AXES)
    placed = (
        P("samp", None, "ty", "tx"),
        P("samp", "ty", "tx"),
        P("samp", None, "ty", "tx"),
        P("samp", "ty", "tx"),
        P("samp", "ty", "tx"),
    )
    return jax.shard_map(
        functools.partial(per_device, sizes),
        mesh=mesh,
        in_specs=placed,
        out_specs=(P(None, "ty", "tx"), P("ty", "tx")),
        check_vma=False,
    )
```

```python
import functools

import jax
import jax.numpy as jnp
from jax import lax
from jax.experimental import pallas as pl
from jax.experimental.pallas import tpu as pltpu
from jax.sharding import PartitionSpec as P

TAPS = (0.0625, 0.25, 0.375, 0.25, 0.0625)
LUMA = (0.2126, 0.7152, 0.0722)
SIGMA_DEPTH = 0.5
SIGMA_NORMAL = 1.0
SIGMA_LUMA = 4.0
LUMA_FLOOR = 0.5
FAR = 1e30

TILE = 128
HALF = 64
RIM = 32
WIN = 96
BLK = 16
AXES = ("samp", "ty", "tx")


def place():
    samp = lax.axis_index("samp")
    ty = lax.axis_index("ty")
    tx = lax.axis_index("tx")
    core = lax.rem(samp, 2)
    y = samp // 2
    half_row = lax.rem(y // 2 + ty, 2)
    half_col = lax.rem(lax.rem(y + 1, 4) // 2 + tx, 2)
    return core, half_row, half_col, ty, tx


def edge_of(core, half_row):
    return lax.rem(core + half_row, 2)


def luminance(c0, c1, c2):
    return LUMA[0] * c0 + LUMA[1] * c1 + LUMA[2] * c2


def rows(start, count):
    return pl.ds(start, count)


def aligned(value):
    return pl.multiple_of(value, 8)


def pick_kernel(wanted, rad, mom, nor, dep, cnt, picked, blocks, sems):
    core = place()[0]
    count = pltpu.make_async_copy(cnt.at[0], blocks, sems.at[4])
    count.start()

    def fill(first, last):
        copies = []
        for ch in range(4):
            source = first.at[0, ch] if ch < 3 else last.at[0]
            copies.append(
                pltpu.make_async_copy(source, picked.at[rows(ch * TILE, TILE), :], sems.at[ch])
            )
        for copy in copies:
            copy.start()
        for copy in copies:
            copy.wait()

    @pl.when(core == wanted)
    def _():
        fill(rad, mom)

    @pl.when(core != wanted)
    def _():
        fill(nor, dep)

    count.wait()
    picked[4 * TILE :, :] = jnp.zeros((8, TILE), jnp.float32)
    picked[4 * TILE :, 0:8] = blocks[...].astype(jnp.float32)


def pair_kernel(keep, recv, *outs):
    _, half_row, half_col, _, _ = place()
    lane = lax.broadcasted_iota(jnp.int32, (HALF, TILE), 1)
    flips = ((0, 0), (0, 1), (1, 1), (1, 0))
    counts = keep[4 * TILE :, :] + recv[4 * TILE :, :]
    for row in range(2):
        total = []
        for ch in range(4):
            at = rows(aligned(ch * TILE + HALF * (half_row if row == 0 else 1 - half_row)), HALF)
            total.append(keep[at, :] + recv[at, :])
        moved = [pltpu.roll(total[3], 96 - 32 * p, 1) for p in range(3)]
        for k in range(4):
            if flips[k][0] == row:
                col = half_col if flips[k][1] == 0 else 1 - half_col
                free = lane // 32 == 3 - 3 * col
                for p in range(3):
                    outs[k][p * HALF : (p + 1) * HALF, :] = jnp.where(free, moved[p], total[p])
                outs[k][3 * HALF :, :] = counts


def mean_kernel(wants_rim, own, r1, r2, r3, out, samples):
    core, half_row, half_col, _, _ = place()
    lane = lax.broadcasted_iota(jnp.int32, (8, TILE), 1)

    def total(at):
        return (own[at, :] + r1[at, :]) + (r2[at, :] + r3[at, :])

    blocks = total(rows(3 * HALF, 8))
    spread = jnp.zeros((8, TILE), jnp.float32)
    for j in range(8):
        spread = jnp.where(lane // BLK == j, blocks[:, j : j + 1], spread)
    samples[...] = spread
    group = lax.broadcasted_iota(jnp.int32, (BLK, TILE), 1) // 32
    for i in range(HALF // BLK):
        count = jnp.broadcast_to(samples[rows(4 * half_row + i, 1), :], (BLK, TILE))
        sums = [total(rows(p * HALF + i * BLK, BLK)) for p in range(3)]
        last = sums[0]
        for p in range(3):
            last = jnp.where(group == p + half_col, pltpu.roll(sums[p], 32 * p + 32, 1), last)
        mean = [value / count for value in (*sums, last)]
        variance = jnp.maximum(mean[3] - jnp.square(luminance(*mean[:3])), 0.0)
        mean[3] = jnp.where(core == 0, variance, mean[3])
        packed = jnp.zeros((BLK, TILE), jnp.float32)
        for ch in range(4):
            if wants_rim:
                moved = pltpu.roll(mean[ch], lax.rem(32 * ch + 32 * half_col, TILE), 1)
                packed = jnp.where(group == ch, moved, packed)
            else:
                out[rows(ch * HALF + i * BLK, BLK), :] = mean[ch]
        if wants_rim:
            out[rows(i * BLK, BLK), :] = packed


def row_kernel(wants_edge, mine, theirs, side, other_side, out):
    core, half_row, half_col, _, tx = place()
    count = RIM if wants_edge else HALF
    first = aligned(32 * edge_of(core, half_row)) if wants_edge else 0
    rim_lane = lax.broadcasted_iota(jnp.int32, (count, TILE), 1) // 32 == 3 * half_col
    outside = rim_lane & (tx == half_col * (lax.axis_size("tx") - 1))

    def fill(colour, normal, colour_rim, normal_rim):
        for g, (field, rims) in enumerate(((colour, colour_rim), (normal, normal_rim))):
            for ch in range(4):
                at = ch * HALF + first
                value = field[rows(aligned(at) if wants_edge else at, count), :]
                value = pltpu.roll(value, 32 + 64 * half_col, 1)
                by = lax.rem(TILE - 32 * ch + 96 * half_col, TILE)
                value = jnp.where(rim_lane, pltpu.roll(rims[rows(first, count), :], by, 1), value)
                if g == 1 and ch == 3:
                    value = jnp.where(outside, FAR, value * (1.0 / SIGMA_DEPTH))
                out[4 * g + ch] = value

    @pl.when(core == 0)
    def _():
        fill(mine, theirs, side, other_side)

    @pl.when(core == 1)
    def _():
        fill(theirs, mine, other_side, side)


MOVES = (-16, -8, -4, -2, -1, 1, 2, 4, 8, 16)


def roll(value, by):
    return pltpu.roll(value, -by % TILE, 1)


def run_level(level, first, last, cur, geo, cur_moved, geo_moved, made, emit):
    dil = 2**level
    for r in range((first - 2 * dil) // 8 * 8, last + 2 * dil, 8):
        at = rows(r, 8)
        for b in (-2, -1, 1, 2):
            if (b * dil, r) not in made:
                made.add((b * dil, r))
                for f in range(4):
                    geo_moved[MOVES.index(b * dil), f, at, :] = roll(geo[f, at, :], b * dil)
            moved = [roll(cur[level, f, at, :], b * dil) for f in range(4)]
            moved.append(luminance(*moved[:3]))
            for f in range(5):
                cur_moved[level, b + 2, f, at, :] = moved[f]

    for r in range(first, last, 8):
        here = rows(r, 8)
        n0, n1, n2, depth = (geo[f, here, :] for f in range(4))
        luma = cur[level, 4, here, :]
        slope = -1.0 / (SIGMA_LUMA * jnp.sqrt(cur[level, 3, here, :]) + LUMA_FLOOR)
        sums = None
        for a in range(-2, 3):
            at = rows(r + a * dil, 8)
            for b in range(-2, 3):
                if b == 0:
                    g = [geo[f, at, :] for f in range(4)]
                    t = [cur[level, f, at, :] for f in range(5)]
                else:
                    g = [geo_moved[MOVES.index(b * dil), f, at, :] for f in range(4)]
                    t = [cur_moved[level, b + 2, f, at, :] for f in range(5)]
                e = jnp.abs(t[4] - luma) * slope - jnp.abs(g[3] - depth)
                e = e - jnp.square(g[0] - n0) - jnp.square(g[1] - n1)
                e = e - jnp.square(g[2] - n2)
                w = (TAPS[a + 2] * TAPS[b + 2]) * jnp.exp(e)
                parts = (w, w * t[0], w * t[1], w * t[2], w * w * t[3])
                sums = parts if sums is None else [p + q for p, q in zip(sums, parts)]
        inv = 1.0 / sums[0]
        emit(r, sums[1] * inv, sums[2] * inv, sums[3] * inv, sums[4] * (inv * inv))


def into(cur, level):
    def emit(r, c0, c1, c2, var):
        for f, value in enumerate((c0, c1, c2, var, luminance(c0, c1, c2))):
            cur[level, f, rows(r, 8), :] = value

    return emit


def place_rows(cur, geo, at, source):
    for f in range(4):
        cur[0, f, at, :] = source[f]
        geo[f, at, :] = source[4 + f]
    cur[0, 4, at, :] = luminance(source[0], source[1], source[2])


INNER = ((4, 60), (8, 56), (16, 48))
OUTER = (
    ((4, 36), (8, 40), (16, 48), (32, 64)),
    ((60, 92), (56, 88), (48, 80), (32, 64)),
)


def inner_kernel(body, near, middle, far, cur, geo, cur_moved, geo_moved):
    core, half_row, _, _, _ = place()
    upper = edge_of(core, half_row) == 0
    place_rows(cur, geo, rows(0, HALF), body)
    made = set()
    for level, (first, last) in enumerate(INNER):
        run_level(
            level, first, last, cur, geo, cur_moved, geo_moved, made, into(cur, level + 1)
        )
    for f in range(5):
        near[f] = jnp.where(upper, cur[1, f, 4:12, :], cur[1, f, 52:60, :])
        middle[f] = jnp.where(upper, cur[2, f, 8:24, :], cur[2, f, 40:56, :])
        far[f] = cur[3, f, 16:48, :]


def outer_kernel(body, edge, near, middle, far, out, cur, geo, cur_moved, geo_moved):
    core, half_row, _, ty, _ = place()

    def work(this):
        outside = (half_row == this) & (ty == (lax.axis_size("ty") - 1 if this else 0))
        place_rows(cur, geo, rows(RIM * (1 - this), HALF), body)
        edge_at = rows(HALF * this, RIM)
        place_rows(cur, geo, edge_at, edge)
        geo[3, edge_at, :] = jnp.where(outside, FAR, edge[7])
        for f in range(5):
            cur[1, f, rows(52 if this else 36, 8), :] = near[f]
            cur[2, f, rows(40, 16), :] = middle[f]
            cur[3, f, rows(16 if this else 48, 32), :] = far[f]
        made = set()

        def finish(r, c0, c1, c2, var):
            lane = lax.broadcasted_iota(jnp.int32, (8, TILE), 1)
            for k, (p, q) in enumerate(((c0, c1), (c2, var))):
                out[rows(k * 32 + r - 32, 8), :] = jnp.where(lane < HALF, roll(p, 32), roll(q, -32))

        for level, (first, last) in enumerate(OUTER[this]):
            emit = into(cur, level + 1) if level < 3 else finish
            run_level(level, first, last, cur, geo, cur_moved, geo_moved, made, emit)

    for this in range(2):
        pl.when(edge_of(core, half_row) == this)(functools.partial(work, this))


def tile_kernel(*refs):
    ins, colour, variance = refs[:8], refs[8], refs[9]
    core, half_row, half_col, _, _ = place()
    lane = lax.broadcasted_iota(jnp.int32, (32, TILE), 1)
    low = lane < HALF
    for side in range(2):
        which = core if side == 0 else 1 - core
        for r in range(2):
            half = half_row if r == 0 else 1 - half_row
            row = aligned(64 * half + 32 * edge_of(which, half))
            near, other = (ins[side * 4 + k] for k in ((0, 1) if r == 0 else (3, 2)))
            for k in range(2):
                p, q = near[k * 32 : (k + 1) * 32, :], other[k * 32 : (k + 1) * 32, :]
                left = jnp.where(half_col == 0, p, q)
                right = jnp.where(half_col == 0, q, p)
                first = jnp.where(low, left, pltpu.roll(right, HALF, 1))
                second = jnp.where(low, pltpu.roll(left, HALF, 1), right)
                at = rows(row, 32)
                colour[2 * k, at, :] = first
                if k == 0:
                    colour[1, at, :] = second
                else:
                    variance[at, :] = second


def estimate(units, levels):
    taps = units * 25 * 8 * TILE
    return pl.CostEstimate(flops=27 * taps, transcendentals=taps, bytes_accessed=levels * 2**16)


def call(kernel, shapes, scratch=(), space=None, cost=None):
    return pl.pallas_call(
        kernel,
        **({"in_specs": [pl.BlockSpec(memory_space=pltpu.HBM)] * space} if space else {}),
        out_shape=[jax.ShapeDtypeStruct(s, jnp.float32) for s in shapes],
        scratch_shapes=list(scratch),
        **({"cost_estimate": estimate(*cost)} if cost else {}),
        compiler_params=pltpu.CompilerParams(vmem_limit_bytes=24 * 2**20),
    )


def run_filter(body, send_edge):
    edge = send_edge()

    def scratch(depth):
        return [
            pltpu.VMEM(shape, jnp.float32)
            for shape in (
                (4, 5, depth, TILE),
                (4, depth, TILE),
                (4, 5, 5, depth, TILE),
                (10, 4, depth, TILE),
            )
        ]

    inner = call(
        inner_kernel, [(5, 8, TILE), (5, 16, TILE), (5, 32, TILE)], scratch(HALF), cost=(17, 3)
    )(body)
    return call(outer_kernel, [(HALF, TILE)], scratch(WIN), cost=(16, 4))(body, edge, *inner)[0]


def pairs(sizes, partner, spare=0):
    n_samp, n_ty, n_tx = sizes

    def flat(samp, ty, tx):
        return (samp * n_ty + ty) * n_tx + tx

    out = []
    for samp in range(n_samp):
        for ty in range(n_ty):
            for tx in range(n_tx):
                to = partner(samp, ty, tx)
                if not (0 <= to[1] < n_ty and 0 <= to[2] < n_tx):
                    to = samp ^ spare, ty, tx
                out.append((flat(samp, ty, tx), flat(*to)))
    return out


def across(samp, ty, tx):
    half_col = ((samp // 2 + 1) % 4 // 2 + tx) % 2
    return samp, ty, tx + (1 if half_col else -1)


def beyond(samp, ty, tx):
    if samp % 2:
        return samp ^ 6, ty, tx
    return samp, ty + (1 if (samp // 4 + ty) % 2 else -1), tx


def per_device(sizes, radiance, moment, normal, depth_sum, counts):
    def send(value, partner, spare=0):
        return lax.ppermute(value, AXES, pairs(sizes, partner, spare))

    def other_core(value):
        return send(value, lambda s, ty, tx: (s ^ 1, ty, tx))

    def other_y(value, k):
        return send(value, lambda s, ty, tx: (s ^ (2 * k), ty, tx))

    packed = (4 * TILE + 8, TILE)
    inputs = [
        pltpu.with_memory_space_constraint(value, pltpu.HBM)
        for value in (radiance, moment, normal, depth_sum, counts)
    ]

    def pick(wanted):
        return call(
            functools.partial(pick_kernel, wanted),
            [packed],
            [pltpu.VMEM((8, 8), jnp.int32), pltpu.SemaphoreType.DMA((5,))],
            5,
            (1, 4),
        )(*inputs)[0]

    give = pick(1)
    keep = pick(0)
    part = (3 * HALF + 8, TILE)
    parts = list(call(pair_kernel, [part] * 4)(keep, other_core(give)))
    parts = parts[:1] + [other_y(parts[k], k) for k in (1, 2, 3)]

    def means(wants_rim):
        return call(
            functools.partial(mean_kernel, wants_rim),
            [(HALF if wants_rim else 4 * HALF, TILE)],
            [pltpu.VMEM((8, TILE), jnp.float32)],
            cost=(1, 4),
        )(*parts)[0]

    rim = means(True)
    mine = means(False)
    theirs = other_core(mine)
    near_rim = send(rim, across, 6)
    cross_rim = send(rim, lambda s, ty, tx: (across(s, ty, tx)[0] ^ 1, *across(s, ty, tx)[1:]), 7)
    sides = (mine, theirs, near_rim, cross_rim)

    def joined(wants_edge, count):
        kernel = functools.partial(row_kernel, wants_edge)
        return call(kernel, [(8, count, TILE)], cost=(1, 8))(*sides)[0]

    edge = send(joined(True, RIM), beyond, 2)
    done = run_filter(joined(False, HALF), lambda: edge)
    got = [done] + [other_y(done, k) for k in (1, 2, 3)]
    theirs = [other_core(g) for g in got]
    return tuple(call(tile_kernel, [(3, TILE, TILE), (TILE, TILE)])(*got, *theirs))


def solution(mesh):
    sizes = tuple(mesh.shape[axis] for axis in AXES)
    placed = (
        P("samp", None, "ty", "tx"),
        P("samp", "ty", "tx"),
        P("samp", None, "ty", "tx"),
        P("samp", "ty", "tx"),
        P("samp", "ty", "tx"),
    )
    return jax.shard_map(
        functools.partial(per_device, sizes),
        mesh=mesh,
        in_specs=placed,
        out_specs=(P(None, "ty", "tx"), P("ty", "tx")),
        check_vma=False,
    )
```
